32 devices in a mesh: groups: 2 (over x), tm: 8 (over z, y), tile: 2 (over core).
Axes of the slice: x: 2, y: 2, z: 4, core: 2. Of those that a mesh axis runs over, the one named last changes fastest.
Arguments:
- frames: bfloat16 [2, 16, 2, 64, 2048], P(None, ('groups', 'tm'), 'tile'), parts along dimension 1, may hold values from -6 to 6
- forward_carry: bfloat16 [16, 2, 64, 2048], P(('groups', 'tm'), 'tile'), parts along dimension 0, may hold values from -6 to 6
- backward_carry: bfloat16 [16, 2, 64, 2048], P(('groups', 'tm'), 'tile'), parts along dimension 0, may hold values from -6 to 6
- forward_source: int32 [2, 16, 32], P(None, ('groups', 'tm'), 'tile'), parts along dimension 1, may hold values from 0 to 31, as said below
- backward_source: int32 [2, 16, 32], P(None, ('groups', 'tm'), 'tile'), parts along dimension 1, may hold values from 0 to 31, as said below
- forward_entry: bfloat16 [9, 64, 128], replicated, may hold values from -0.1875 to 0.1875
- forward_blocks: bfloat16 [1, 2, 9, 64, 64], replicated, may hold values from -0.25 to 0.25
- backward_entry: bfloat16 [9, 64, 128], replicated, may hold values from -0.1875 to 0.1875
- backward_blocks: bfloat16 [1, 2, 9, 64, 64], replicated, may hold values from -0.25 to 0.25
- mixing_weight: bfloat16 [64, 128], replicated, may hold values from -0.5 to 0.5
Outputs:
- restored: bfloat16 [2, 16, 2, 64, 2048], P(None, ('groups', 'tm'), 'tile'), parts along dimension 1
- forward_final: bfloat16 [16, 2, 64, 2048], P(('groups', 'tm'), 'tile'), parts along dimension 0
- backward_final: bfloat16 [16, 2, 64, 2048], P(('groups', 'tm'), 'tile'), parts along dimension 0
The draws below stay inside these ranges and needn't reach their ends.
There are 2 independent parts, one for each index of `groups`. The reference program is written for one: setup_inputs(seed, part) draws one part's arguments, and reference() takes and returns one part's arrays. A program takes and returns all parts, laid end to end along the dimension named above; an argument that names none is the same for every part. Nothing has to cross between parts.
Inputs may be any that keep to these rules, and one draw needn't show every extreme that they name: `forward_source`: for each step, segment and destination block of a frame, the block whose forward features it takes: the destination moved by at most one block row and three block columns, kept inside the frame. `backward_source`: the same for backward features.
All inputs are finite; a program needn't handle non-finite values.
Results may differ from the reference program's by a relative error of at most 0.012.
Values may be sent and summed in bfloat16 or wider, within the bound.
No kernel may reach another device: no remote copies, remote signals or barrier semaphores. Data moves between devices by JAX's collectives and lax.ppermute only.
A program may use at most 64 MiB of HBM per device.

```python
import jax
import jax.numpy as jnp
from jax import lax

C = 64
RH = 32
RW = 64
BH = 8
BW = 16
NB = 1
TICKS = 2
SEGMENTS = 8
NREG = 2
BLOCKS = 32


def source_draw(key):
    block_rows = RH // BH
    block_cols = RW // BW
    per_region = block_rows * block_cols
    positions = jnp.arange(BLOCKS, dtype=jnp.int32)
    region = positions // per_region
    within = positions % per_region
    dest_row = within // block_cols
    dest_col = region * block_cols + within % block_cols
    row_key, col_key = jax.random.split(key)
    draw_shape = (TICKS, SEGMENTS, BLOCKS)
    row_move = jax.random.randint(row_key, draw_shape, -1, 2).astype(jnp.int32)
    col_move = jax.random.randint(col_key, draw_shape, -3, 4).astype(jnp.int32)
    final_block = positions == BLOCKS - 1
    start_block = positions == 0
    row_move = jnp.where(final_block, jnp.abs(row_move), jnp.where(start_block, -jnp.abs(row_move), row_move))
    col_move = jnp.where(final_block, jnp.abs(col_move), jnp.where(start_block, -jnp.abs(col_move), col_move))
    src_row = jnp.clip(dest_row + row_move, 0, block_rows - 1)
    src_col = jnp.clip(dest_col + col_move, 0, NREG * block_cols - 1)
    return (src_col // block_cols * per_region + src_row * block_cols + src_col % block_cols).astype(jnp.int32)


def draw_forward_source(key, part):
    return source_draw(jax.random.fold_in(key, 11))


def draw_backward_source(key, part):
    return source_draw(jax.random.fold_in(key, 23))


def level_of(rng, extent, shards, smallest, largest):
    gain = 1.0
    for dim, shards_of in shards:
        steps = jax.random.uniform(jax.random.fold_in(jax.random.fold_in(rng, 6), dim), (shards_of,), jnp.float32, smallest / len(shards), largest / len(shards))
        gain = gain * jnp.repeat(jnp.exp(steps), extent[dim] // shards_of).reshape((-1,) + (1,) * (len(extent) - 1 - dim))
    return gain


def noise(stream_key, dims, width, reach, cuts=(), kind=jnp.bfloat16):
    drawn = jax.random.normal(stream_key, dims, jnp.float32) * width
    if len(cuts) > 0:
        drawn = level_of(stream_key, dims, cuts, -0.22, 0.18) * drawn
    return jnp.clip(drawn, min=-reach, max=reach).astype(kind)


def setup_inputs(seed: int = 0, part: int = 0) -> dict:
    key_list = jax.random.split(jax.random.key(seed), 11)
    part_keys = jax.random.split(jax.random.fold_in(key_list[10], part), 11)
    return {
        "frames": noise(part_keys[0], (TICKS, SEGMENTS, NREG, C, RH * RW), 1.0, 6.0, ((1, 8), (2, 2))),
        "forward_carry": noise(part_keys[1], (SEGMENTS, NREG, C, RH * RW), 1.0, 6.0, ((0, 8), (1, 2))),
        "backward_carry": noise(part_keys[2], (SEGMENTS, NREG, C, RH * RW), 1.0, 6.0, ((0, 8), (1, 2))),
        "forward_source": draw_forward_source(jax.random.fold_in(jax.random.fold_in(key_list[10], part), 71), part),
        "backward_source": draw_backward_source(jax.random.fold_in(jax.random.fold_in(key_list[10], part), 71), part),
        "forward_entry": noise(key_list[5], (9, C, 2 * C), (18 * C) ** -0.5, 0.1875),
        "forward_blocks": noise(key_list[6], (NB, 2, 9, C, C), (9 * C) ** -0.5, 0.25),
        "backward_entry": noise(key_list[7], (9, C, 2 * C), (18 * C) ** -0.5, 0.1875),
        "backward_blocks": noise(key_list[8], (NB, 2, 9, C, C), (9 * C) ** -0.5, 0.25),
        "mixing_weight": noise(key_list[9], (C, 2 * C), (2 * C) ** -0.5, 0.5),
    }


def convolve(feature, weight):
    regions, channels, pixels = feature.shape
    grid = feature.astype(jnp.float32).reshape(regions, channels, RH, RW)
    padded = jnp.pad(grid, ((0, 0), (0, 0), (1, 1), (1, 1)))
    summed = jnp.zeros((regions, weight.shape[1], pixels), jnp.float32)
    for kernel_tap in range(9):
        row_off = kernel_tap // 3
        col_off = kernel_tap % 3
        window = padded[:, :, row_off:row_off + RH, col_off:col_off + RW].reshape(regions, channels, pixels)
        summed = summed + jnp.einsum("oi,rip->rop", weight[kernel_tap].astype(jnp.float32), window, precision=lax.Precision.HIGHEST)
    return summed


def to_blocks(feature):
    regions, channels, pixels = feature.shape
    grid = feature.reshape(regions, channels, RH // BH, BH, RW // BW, BW)
    grid = grid.transpose(0, 2, 4, 1, 3, 5)
    return grid.reshape(regions * (RH // BH) * (RW // BW), channels, BH * BW)


def from_blocks(blocks, regions):
    channels = blocks.shape[1]
    grid = blocks.reshape(regions, RH // BH, RW // BW, channels, BH, BW)
    grid = grid.transpose(0, 3, 1, 4, 2, 5)
    return grid.reshape(regions, channels, RH * RW)


def warp_blocks(whole_frame, sources):
    per_region = (RH // BH) * (RW // BW)
    picked = jnp.take(to_blocks(whole_frame), sources, axis=0)
    return from_blocks(picked, sources.shape[0] // per_region)


def propagate(frame_now, warped, entry, layers):
    joined = jnp.concatenate([frame_now, warped], axis=1)
    hidden = jax.nn.leaky_relu(convolve(joined, entry), 0.1).astype(jnp.bfloat16)
    for layer in range(layers.shape[0]):
        inner = jax.nn.leaky_relu(convolve(hidden, layers[layer, 0]), 0.1).astype(jnp.bfloat16)
        hidden = (hidden.astype(jnp.float32) + convolve(inner, layers[layer, 1])).astype(jnp.bfloat16)
    return hidden


def reference(frames, forward_carry, backward_carry, forward_source, backward_source, forward_entry, forward_blocks, backward_entry, backward_blocks, mixing_weight):
    forward_state = forward_carry
    backward_state = backward_carry
    segments, regions, channels, pixels = forward_carry.shape
    results = []
    for moment in range(TICKS):
        frame_now = frames[moment].reshape(segments * regions, channels, pixels)
        empty = jnp.zeros_like(forward_state[:1])
        came_forward = jnp.concatenate([empty, forward_state[:-1]], axis=0)
        came_backward = jnp.concatenate([backward_state[1:], empty], axis=0)
        warped_forward = jax.vmap(warp_blocks)(came_forward, forward_source[moment])
        warped_backward = jax.vmap(warp_blocks)(came_backward, backward_source[moment])
        new_forward = propagate(frame_now, warped_forward.reshape(segments * regions, channels, pixels), forward_entry, forward_blocks)
        new_backward = propagate(frame_now, warped_backward.reshape(segments * regions, channels, pixels), backward_entry, backward_blocks)
        both = jnp.concatenate([new_forward, new_backward], axis=1).astype(jnp.float32)
        mixed = jnp.einsum("oi,rip->rop", mixing_weight.astype(jnp.float32), both, precision=lax.Precision.HIGHEST)
        results.append((frame_now.astype(jnp.float32) + mixed).astype(jnp.bfloat16).reshape(segments, regions, channels, pixels))
        forward_state = new_forward.reshape(segments, regions, channels, pixels)
        backward_state = new_backward.reshape(segments, regions, channels, pixels)
    return jnp.stack(results), forward_state, backward_state
```

```python
import functools

import jax
import jax.numpy as jnp
from jax import lax
from jax.experimental import pallas as pl
from jax.experimental.pallas import tpu as pltpu
from jax.sharding import PartitionSpec as P

RH = 32
RW = 64
BH = 8
BW = 16
LANES = 128
GROUPS = RH * RW // LANES
BLOCK_ROWS = RH // BH
BLOCK_COLS = RW // BW
BF16 = jnp.bfloat16


def lane_of(shape):
    return lax.broadcasted_iota(jnp.int32, shape, 1)


def split_groups(groups):
    low = lane_of(groups[0].shape) < RW
    out = []
    for v in range(GROUPS // 2):
        top, bottom = groups[v], groups[v + GROUPS // 2]
        out.append(jnp.where(low, top, pltpu.roll(bottom, RW, 1)))
        out.append(jnp.where(low, pltpu.roll(top, RW, 1), bottom))
    return out


def natural_groups(groups):
    low = lane_of(groups[0].shape) < RW
    top, bottom = [], []
    for v in range(GROUPS // 2):
        first, second = groups[2 * v], groups[2 * v + 1]
        top.append(jnp.where(low, first, pltpu.roll(second, RW, 1)))
        bottom.append(jnp.where(low, pltpu.roll(first, RW, 1), second))
    return top + bottom


def load_groups(ref):
    return [ref[:, v * LANES : (v + 1) * LANES] for v in range(GROUPS)]


def store_groups(ref, groups):
    for v, group in enumerate(groups):
        ref[:, v * LANES : (v + 1) * LANES] = group


def selection(index_ref):
    halves = GROUPS // BH
    lane = lane_of((1, LANES))
    depth = 2 * halves * LANES
    row = lax.broadcasted_iota(jnp.int32, (depth, LANES), 0)
    columns = []
    for group in range(halves):
        target = jnp.zeros((1, LANES), jnp.int32)
        for piece in range(LANES // BW):
            half, col = piece // BLOCK_COLS, piece % BLOCK_COLS
            source = index_ref[(group + halves * half) * BLOCK_COLS + col]
            tile, local = source // (BLOCK_ROWS * BLOCK_COLS), source % (BLOCK_ROWS * BLOCK_COLS)
            block_row, block_col = local // BLOCK_COLS, local % BLOCK_COLS
            base = (tile * halves + block_row % halves) * LANES + block_row // halves * RW + block_col * BW
            target = jnp.where(lane // BW == piece, base + lane % BW, target)
        columns.append((row == target).astype(jnp.float32).astype(BF16))
    return jnp.concatenate(columns, axis=1)


def warp(first, second, chosen):
    halves = GROUPS // BH
    channels = first[0].shape[0]
    rows = []
    for i in range(BH):
        rows.append(
            jnp.concatenate([t[BH * g + i] for t in (first, second) for g in range(halves)], axis=1)
        )
    picked = jnp.dot(jnp.concatenate(rows, axis=0), chosen, preferred_element_type=jnp.float32).astype(BF16)
    return [
        picked[i * channels : (i + 1) * channels, g * LANES : (g + 1) * LANES]
        for g in range(halves)
        for i in range(BH)
    ]


def put_taps(stack, bases, groups):
    channels = groups[0].shape[0]
    lane = lane_of(groups[0].shape)
    zero = jnp.zeros_like(groups[0])
    above = jnp.where(lane < RW, zero, pltpu.roll(groups[-1], RW, 1))
    below = jnp.where(lane < RW, pltpu.roll(groups[0], RW, 1), zero)
    for v, group in enumerate([above] + groups + [below]):
        before = jnp.where(lane % RW == 0, zero, pltpu.roll(group, 1, 1))
        after = jnp.where(lane % RW == RW - 1, zero, pltpu.roll(group, LANES - 1, 1))
        for base, value in zip(bases, (before, group, after)):
            stack[base : base + channels, v * LANES : (v + 1) * LANES] = value


def convolve(stack, weight):
    channels = weight.shape[0] // 3
    depth = weight.shape[1]
    parts = []
    out = []
    for t in range(GROUPS // 2 + 1):
        wide = jnp.dot(
            weight, stack[:depth, 2 * t * LANES : 2 * (t + 1) * LANES], preferred_element_type=jnp.float32
        )
        parts += [wide[:, :LANES], wide[:, LANES:]]
        if t > 0:
            for r in (2 * t - 2, 2 * t - 1):
                out.append(
                    parts[r][:channels]
                    + parts[r + 1][channels : 2 * channels]
                    + parts[r + 2][2 * channels :]
                )
    return out


def weight_of(ref):
    return jnp.concatenate(
        [jnp.concatenate([ref[3 * a + b] for b in range(3)], axis=1) for a in range(3)], axis=0
    )


def lrelu(groups):
    return [jnp.maximum(u, 0.1 * u).astype(BF16) for u in groups]


def propagate(stack, frame, warped, entry, layers):
    channels = frame[0].shape[0]
    put_taps(stack, [2 * b * channels for b in range(3)], frame)
    put_taps(stack, [(2 * b + 1) * channels for b in range(3)], warped)
    hidden = lrelu(convolve(stack, weight_of(entry)))
    bases = [b * channels for b in range(3)]
    for layer in range(layers.shape[0]):
        put_taps(stack, bases, hidden)
        inner = lrelu(convolve(stack, weight_of(layers.at[layer, 0])))
        put_taps(stack, bases, inner)
        update = convolve(stack, weight_of(layers.at[layer, 1]))
        hidden = [(h.astype(jnp.float32) + u).astype(BF16) for h, u in zip(hidden, update)]
    return hidden


def tick(
    forward_index,
    backward_index,
    frame,
    forward_whole,
    backward_whole,
    forward_entry,
    forward_blocks,
    backward_entry,
    backward_blocks,
    mixing,
    restored,
    forward_out,
    backward_out,
    forward_stack,
    backward_stack,
):
    frame_groups = load_groups(frame)
    frame_split = split_groups(frame_groups)
    finals = []
    for index, whole, entry, layers, out, stack in (
        (forward_index, forward_whole, forward_entry, forward_blocks, forward_out, forward_stack),
        (backward_index, backward_whole, backward_entry, backward_blocks, backward_out, backward_stack),
    ):
        tiles = [split_groups(load_groups(whole.at[t])) for t in range(2)]
        warped = warp(tiles[0], tiles[1], selection(index))
        final = natural_groups(propagate(stack, frame_split, warped, entry, layers))
        store_groups(out, final)
        finals.append(final)
    for v in range(0, GROUPS, 2):
        both = jnp.concatenate([jnp.concatenate(f[v : v + 2], axis=1) for f in finals], axis=0)
        mixed = jnp.dot(mixing[...], both, preferred_element_type=jnp.float32)
        here = jnp.concatenate(frame_groups[v : v + 2], axis=1).astype(jnp.float32)
        restored[:, v * LANES : (v + 2) * LANES] = (here + mixed).astype(BF16)


def run_tick(forward_index, backward_index, frame, *rest):
    channels, pixels = frame.shape
    smem = pl.BlockSpec(memory_space=pltpu.SMEM)
    vmem = pl.BlockSpec(memory_space=pltpu.VMEM)
    shape = jax.ShapeDtypeStruct((channels, pixels), BF16)
    stack = pltpu.VMEM((6 * channels, (GROUPS + 2) * LANES), BF16)
    flops = 2 * 2 * pixels * channels * channels * 36
    return pl.pallas_call(
        tick,
        out_shape=(shape, shape, shape),
        in_specs=[smem, smem] + [vmem] * (1 + len(rest)),
        out_specs=(vmem, vmem, vmem),
        scratch_shapes=[stack, stack],
        compiler_params=pltpu.CompilerParams(vmem_limit_bytes=32 * 2**20),
        cost_estimate=pl.CostEstimate(flops=flops, bytes_accessed=4 * 2**20, transcendentals=0),
        name="tick",
    )(forward_index, backward_index, frame, *rest)


def passed_along(value, axis, steps):
    count = lax.axis_size(axis)
    leading, last = (max(0, -steps), min(count, count - steps))
    return lax.ppermute(value, axis, [(source, source + steps) for source in range(leading, last)])


def shards(
    frames,
    forward_carry,
    backward_carry,
    forward_source,
    backward_source,
    forward_entry,
    forward_blocks,
    backward_entry,
    backward_blocks,
    mixing_weight,
):
    forward_state = forward_carry[0]
    backward_state = backward_carry[0]
    results = []
    for moment in range(frames.shape[0]):
        came_forward = passed_along(forward_state, "tm", 1)
        came_backward = passed_along(backward_state, "tm", -1)
        whole_forward = lax.all_gather(came_forward, "tile", axis=0, tiled=True)
        whole_backward = lax.all_gather(came_backward, "tile", axis=0, tiled=True)
        restored, forward_now, backward_now = run_tick(
            forward_source[moment, 0],
            backward_source[moment, 0],
            frames[moment, 0, 0],
            whole_forward,
            whole_backward,
            forward_entry,
            forward_blocks,
            backward_entry,
            backward_blocks,
            mixing_weight,
        )
        forward_state, backward_state = forward_now[None], backward_now[None]
        results.append(restored)
    restored = jnp.stack(results)[:, None, None]
    return (restored, forward_state[None], backward_state[None])


def solution(mesh):
    placed = (
        P(None, ("groups", "tm"), "tile", None, None),
        P(("groups", "tm"), "tile", None, None),
        P(("groups", "tm"), "tile", None, None),
        P(None, ("groups", "tm"), "tile"),
        P(None, ("groups", "tm"), "tile"),
        P(),
        P(),
        P(),
        P(),
        P(),
    )
    return jax.shard_map(
        shards,
        mesh=mesh,
        in_specs=placed,
        out_specs=(
            P(None, ("groups", "tm"), "tile", None, None),
            P(("groups", "tm"), "tile", None, None),
            P(("groups", "tm"), "tile", None, None),
        ),
        check_vma=False,
    )
```

```python
import functools

import jax
import jax.numpy as jnp
from jax import lax
from jax.experimental import pallas as pl
from jax.experimental.pallas import tpu as pltpu
from jax.sharding import PartitionSpec as P

RH = 32
RW = 64
BH = 8
BW = 16
LANES = 128
BLOCK_ROWS = RH // BH
BLOCK_COLS = RW // BW
REGION_BLOCKS = BLOCK_ROWS * BLOCK_COLS
PAIRS = RW // 2
BLOCK_PAIRS = BW // 2
NATURAL = RH * RW // LANES
ROWS_IN_GROUP = LANES // RW
QUADS = BH // ROWS_IN_GROUP
BF16 = jnp.bfloat16
F32 = jnp.float32


def lanes(shape):
    return lax.broadcasted_iota(jnp.int32, shape, len(shape) - 1)


def cut(value, count):
    return [value[:, v * LANES : (v + 1) * LANES] for v in range(count)]


def one_hot(depth, target):
    row = lax.broadcasted_iota(jnp.int32, (depth, target.shape[1]), 0)
    return (row == target).astype(F32).astype(BF16)


def dot(a, b):
    return jnp.dot(a, b, preferred_element_type=F32)


def pairing():
    width = BLOCK_ROWS * LANES
    n = lanes((1, width))
    parity = n // LANES
    target = n % LANES // PAIRS * LANES + parity // 2 * RW + n % PAIRS * 2 + parity % 2
    return one_hot(width, target)


def to_paired(groups, matrix):
    channels = groups[0].shape[0]
    rows = [
        jnp.concatenate([groups[QUADS * br + j] for br in range(BLOCK_ROWS)], axis=1) for j in range(QUADS)
    ]
    moved = dot(jnp.concatenate(rows, axis=0), matrix).astype(BF16)
    out = []
    for j in range(QUADS):
        here = cut(moved[j * channels : (j + 1) * channels], BLOCK_ROWS)
        for q in range(ROWS_IN_GROUP):
            out.append(jnp.concatenate(here[2 * q : 2 * q + 2], axis=0))
    return out


def unpairing():
    width = BLOCK_ROWS * LANES
    n = lanes((1, width))
    column = n % RW
    target = (n % LANES // RW * 2 + column % 2) * LANES + n // LANES * PAIRS + column // 2
    return one_hot(width, target)


def to_natural(maps, matrix):
    channels = maps[0][0].shape[0] // 2
    rows = []
    for groups in maps:
        for j in range(QUADS):
            parts = []
            for q in range(ROWS_IN_GROUP):
                group = groups[ROWS_IN_GROUP * j + q]
                parts += [group[:channels], group[channels:]]
            rows.append(jnp.concatenate(parts, axis=1))
    moved = dot(jnp.concatenate(rows, axis=0), matrix).astype(BF16)
    out = []
    for m in range(len(maps)):
        here = [
            cut(moved[(m * QUADS + j) * channels : (m * QUADS + j + 1) * channels], BLOCK_ROWS)
            for j in range(QUADS)
        ]
        out.append([here[j][br] for br in range(BLOCK_ROWS) for j in range(QUADS)])
    return out


def lane_target(source, tile):
    slot = (source // REGION_BLOCKS + tile) % 2
    return slot * LANES + source % REGION_BLOCKS * BLOCK_PAIRS


def spread(index):
    row = lax.broadcasted_iota(jnp.int32, (REGION_BLOCKS, LANES), 0)
    places = (row == lanes((REGION_BLOCKS, LANES)) // BLOCK_PAIRS).astype(F32).astype(BF16)
    rows = jnp.broadcast_to(index.astype(F32), (REGION_BLOCKS, REGION_BLOCKS)).astype(BF16)
    return dot(rows, places)


def target_of(source, tile):
    return lane_target(source.astype(jnp.int32), tile) + lanes((1, LANES)) % BLOCK_PAIRS


def add_halo(stack):
    shape = (stack.shape[0], LANES)
    lane = lanes(shape)
    zero = jnp.zeros(shape, BF16)
    last = pltpu.roll(stack[:, BH * LANES : (BH + 1) * LANES], PAIRS, 1)
    first = pltpu.roll(stack[:, LANES : 2 * LANES], LANES - PAIRS, 1)
    stack[:, :LANES] = jnp.where(lane < PAIRS, zero, last)
    stack[:, (BH + 1) * LANES :] = jnp.where(lane >= LANES - PAIRS, zero, first)


def put_taps(stack, groups):
    channels = groups[0].shape[0] // 2
    shape = (channels, LANES)
    lane = lanes(shape)
    zero = jnp.zeros(shape, BF16)
    for i, group in enumerate(groups):
        columns = slice((i + 1) * LANES, (i + 2) * LANES)
        before = pltpu.roll(group[channels:], 1, 1)
        after = pltpu.roll(group[:channels], LANES - 1, 1)
        stack[channels : 3 * channels, columns] = group
        stack[:channels, columns] = jnp.where(lane % PAIRS == 0, zero, before)
        stack[3 * channels :, columns] = jnp.where(lane % PAIRS == PAIRS - 1, zero, after)
    add_halo(stack)


def put_warped(stack, own, other, target):
    channels = own.shape[0] // 2
    lane = lanes((1, LANES))
    before = jnp.where(lane % PAIRS == 0, -1, pltpu.roll(target, 1, 1))
    after = jnp.where(lane % PAIRS == PAIRS - 1, -1, pltpu.roll(target, LANES - 1, 1))
    depth = 2 * LANES
    even_pick = one_hot(depth, jnp.concatenate([target, after], axis=1))
    odd_pick = one_hot(depth, jnp.concatenate([before, target], axis=1))
    for rows, pick, places in (
        (slice(0, channels), even_pick, (1, 3)),
        (slice(channels, 2 * channels), odd_pick, (0, 2)),
    ):
        wide = [
            jnp.concatenate(
                [own[rows, i * LANES : (i + 1) * LANES], other[rows, i * LANES : (i + 1) * LANES]], axis=1
            )
            for i in range(BH)
        ]
        moved = dot(jnp.concatenate(wide, axis=0), pick).astype(BF16)
        for i in range(BH):
            columns = slice((i + 1) * LANES, (i + 2) * LANES)
            for half, place in enumerate(places):
                stack[place * channels : (place + 1) * channels, columns] = moved[
                    i * channels : (i + 1) * channels, half * LANES : (half + 1) * LANES
                ]
    add_halo(stack)


def convolve(stack, weight, start=None):
    out = []
    for t in range(0, BH, 2):
        total = None if start is None else start[:, t * LANES : (t + 2) * LANES]
        for a in range(3):
            part = dot(weight[a], stack[:, (t + a) * LANES : (t + a + 2) * LANES])
            total = part if total is None else total + part
        out += cut(total, 2)
    return out


def lrelu(groups):
    return [jnp.maximum(u, 0.1 * u).astype(BF16) for u in groups]


def chains(stacks, entry, starts, layers):
    both = range(2)
    hidden = [lrelu(convolve(stacks[d], entry.at[d], starts[d])) for d in both]
    for layer in range(layers.shape[1]):
        for d in both:
            put_taps(stacks[d], hidden[d])
        inner = [lrelu(convolve(stacks[d], layers.at[d, layer, 0])) for d in both]
        for d in both:
            put_taps(stacks[d], inner[d])
        update = [convolve(stacks[d], layers.at[d, layer, 1]) for d in both]
        hidden = [[(h.astype(F32) + u).astype(BF16) for h, u in zip(hidden[d], update[d])] for d in both]
    return hidden


def even_segment():
    return lax.axis_index("tm") % 2 == 0


def head_kernel(frames, forward_index, backward_index, payload, index, sem, index_sems):
    channels, pixels = frames.shape[-2:]
    copies = [pltpu.make_async_copy(frames.at[0, 0, 0], payload.at[:, :pixels], sem)]
    for d, source in enumerate((forward_index, backward_index)):
        copies.append(pltpu.make_async_copy(source, index.at[d], index_sems.at[d]))
    for copy in copies:
        copy.start()
    half = channels // 2
    for d in range(2):
        copies[1 + d].wait()
        source = spread(index[d, 0]).astype(BF16)
        for row in range(d * half, (d + 1) * half, REGION_BLOCKS):
            payload[row : row + REGION_BLOCKS, pixels:] = source
    copies[0].wait()


def pack_kernel(forward, backward, near_out, far_out):
    matrix = pairing()
    even = even_segment()
    packed = [to_paired(cut(source[0, 0], NATURAL), matrix) for source in (forward, backward)]
    for i, (f, b) in enumerate(zip(*packed)):
        columns = slice(i * LANES, (i + 1) * LANES)
        near_out[:, columns] = jnp.where(even, f, b)
        far_out[:, columns] = jnp.where(even, b, f)


def frame_kernel(frames, entry_frame, *rest):
    outs, stack = rest[:-1], rest[-1]
    matrix = pairing()
    channels = frames.shape[-2]
    for moment, out in enumerate(outs):
        put_taps(stack, to_paired(cut(frames[moment, 0, 0], NATURAL), matrix))
        for i, group in enumerate(convolve(stack, entry_frame)):
            for d in range(2):
                out[d, :, i * LANES : (i + 1) * LANES] = group[2 * d * channels : 2 * (d + 1) * channels]


def tap_weight(taps):
    zero = jnp.zeros_like(taps[0])
    return jnp.concatenate(
        [jnp.concatenate(taps + [zero], axis=1), jnp.concatenate([zero] + taps, axis=1)], axis=0
    )


def weights_kernel(fe, fb, be, bb, entry_frame, entry_warped, layers):
    channels = fe.shape[1]
    for d, (entry, blocks) in enumerate(((fe, fb), (be, bb))):
        for a in range(3):
            taps = [entry[3 * a + b] for b in range(3)]
            entry_frame[a, 2 * d * channels : 2 * (d + 1) * channels] = tap_weight(
                [t[:, :channels] for t in taps]
            )
            entry_warped[d, a] = tap_weight([t[:, channels:] for t in taps])
            for layer in range(blocks.shape[0]):
                for part in range(2):
                    layers[d, layer, part, a] = tap_weight(
                        [blocks[layer, part, 3 * a + b] for b in range(3)]
                    )


def by_direction(even, pair_side, other_side):
    first, second = pair_side[...], other_side[...]
    return jnp.where(even, second, first), jnp.where(even, first, second)


def near_frame_kernel(pair_frame, other_frame, entry_frame, out, lists, stack):
    matrix = pairing()
    even = even_segment()
    width = NATURAL * LANES
    channels = pair_frame.shape[0]
    half = channels // 2
    payloads = by_direction(even, pair_frame, other_frame)
    for d in range(2):
        put_taps(stack.at[d], to_paired(cut(payloads[d][:, :width], NATURAL), matrix))
        lists[d] = payloads[d][d * half : (d + 1) * half, width:]
    for d in range(2):
        weight = [entry_frame[a, 2 * d * channels : 2 * (d + 1) * channels] for a in range(3)]
        for i, group in enumerate(convolve(stack.at[d], weight)):
            out[d, :, i * LANES : (i + 1) * LANES] = group


def near_kernel(
    pair_own,
    pair_swapped,
    other_own,
    other_swapped,
    starts,
    lists,
    entry_warped,
    layers,
    forward_out,
    backward_out,
    forward_stack,
    backward_stack,
):
    even = even_segment()
    tile = lax.axis_index("tile")
    stacks = (forward_stack, backward_stack)
    owns = by_direction(even, pair_own, other_own)
    others = by_direction(even, pair_swapped, other_swapped)
    for d in range(2):
        source = lists[d].astype(F32)[:1]
        put_warped(stacks[d], owns[d], others[d], target_of(source, tile))
    hidden = chains(stacks, entry_warped, [starts.at[d] for d in range(2)], layers)
    for groups, out in zip(hidden, (forward_out, backward_out)):
        for i, group in enumerate(groups):
            out[:, i * LANES : (i + 1) * LANES] = group


def tick_kernel(
    moment,
    forward_index,
    backward_index,
    frames,
    first_own,
    first_swapped,
    second_own,
    second_swapped,
    starts,
    entry_warped,
    layers,
    mixing,
    *rest,
):
    *_, restored, forward_final, backward_final = rest[:-6] if moment > 0 else rest[:-6] + (None, None)
    forward_stack, backward_stack, finals, mixed, final_sems, mixed_sems = rest[-6:]
    stacks = (forward_stack, backward_stack)
    back = unpairing()
    tile = lax.axis_index("tile")
    owns, others = (first_own[...], second_own[...]), (first_swapped[...], second_swapped[...])
    if moment == 0:
        even = even_segment()
        owns = by_direction(even, first_own, second_own)
        others = by_direction(even, first_swapped, second_swapped)
    for d, index in enumerate((forward_index, backward_index)):
        put_warped(stacks[d], owns[d], others[d], target_of(spread(index[moment])[:1], tile))
    hidden = chains(stacks, entry_warped, [starts.at[d] for d in range(2)], layers)
    states = to_natural(hidden, back)
    copies = []
    if moment > 0:
        for d, out in enumerate((forward_final, backward_final)):
            for v, group in enumerate(states[d]):
                finals[d, :, v * LANES : (v + 1) * LANES] = group
            copies.append(pltpu.make_async_copy(finals.at[d], out, final_sems.at[d]))
            copies[-1].start()
    for part in range(2):
        count = NATURAL // 2
        for v in range(part * count, (part + 1) * count, 2):
            both = jnp.concatenate([jnp.concatenate(f[v : v + 2], axis=1) for f in states], axis=0)
            here = frames[moment, 0, 0, :, v * LANES : (v + 2) * LANES].astype(F32)
            mixed[:, v * LANES : (v + 2) * LANES] = (here + dot(mixing[...], both)).astype(BF16)
        columns = pl.ds(part * count * LANES, count * LANES)
        copies.append(
            pltpu.make_async_copy(mixed.at[:, columns], restored.at[moment, :, columns], mixed_sems.at[part])
        )
        copies[-1].start()
    for copy in copies:
        copy.wait()


VMEM = pl.BlockSpec(memory_space=pltpu.VMEM)
ANY = pl.BlockSpec(memory_space=pl.ANY)
PARAMS = pltpu.CompilerParams(vmem_limit_bytes=32 * 2**20)


def cost(flops, count):
    return pl.CostEstimate(flops=flops, bytes_accessed=count, transcendentals=0)


def head(frames, forward_source, backward_source):
    channels, pixels = frames.shape[-2:]
    return pl.pallas_call(
        head_kernel,
        out_shape=jax.ShapeDtypeStruct((channels, pixels + LANES), BF16),
        in_specs=[ANY] * 3,
        out_specs=VMEM,
        scratch_shapes=[
            pltpu.VMEM((2,) + forward_source.shape, jnp.int32),
            pltpu.SemaphoreType.DMA,
            pltpu.SemaphoreType.DMA((2,)),
        ],
        compiler_params=pltpu.CompilerParams(vmem_limit_bytes=60 * 2**20),
        cost_estimate=cost(2**30, 2**19),
        name="head",
    )(frames, forward_source, backward_source)


def pack(forward, backward):
    channels, pixels = forward.shape[-2:]
    shape = jax.ShapeDtypeStruct((2 * channels, pixels // 2), BF16)
    return pl.pallas_call(
        pack_kernel,
        out_shape=(shape, shape),
        in_specs=[VMEM] * 2,
        out_specs=(VMEM, VMEM),
        compiler_params=PARAMS,
        cost_estimate=cost(2**29, 2**19),
        name="pack",
    )(forward, backward)


def pair_weights(forward_entry, forward_blocks, backward_entry, backward_blocks):
    channels = forward_entry.shape[1]
    count = forward_blocks.shape[0]
    matrix = (2 * channels, 4 * channels)
    return pl.pallas_call(
        weights_kernel,
        out_shape=(
            jax.ShapeDtypeStruct((3, 4 * channels, 4 * channels), BF16),
            jax.ShapeDtypeStruct((2, 3) + matrix, BF16),
            jax.ShapeDtypeStruct((2, count, 2, 3) + matrix, BF16),
        ),
        in_specs=[VMEM] * 4,
        out_specs=(VMEM,) * 3,
        compiler_params=PARAMS,
        cost_estimate=cost(2**28, 2**19),
        name="pair_weights",
    )(forward_entry, forward_blocks, backward_entry, backward_blocks)


def stack_of(channels):
    return pltpu.VMEM((4 * channels, (BH + 2) * LANES), BF16)


def frame_parts(frames, entry_frame):
    channels, pixels = frames.shape[-2:]
    part = jax.ShapeDtypeStruct((2, 2 * channels, pixels // 2), F32)
    return pl.pallas_call(
        frame_kernel,
        out_shape=(part,) * frames.shape[0],
        in_specs=[VMEM] * 2,
        out_specs=(VMEM,) * frames.shape[0],
        scratch_shapes=[stack_of(channels)],
        compiler_params=PARAMS,
        cost_estimate=cost(2**31, 2**19),
        name="frame_parts",
    )(frames, entry_frame)


def near_frames(pair_frame, other_frame, entry_frame):
    channels, width = pair_frame.shape
    stack = stack_of(channels)
    return pl.pallas_call(
        near_frame_kernel,
        out_shape=(
            jax.ShapeDtypeStruct((2, 2 * channels, (width - LANES) // 2), F32),
            jax.ShapeDtypeStruct((2, channels // 2, LANES), BF16),
        ),
        in_specs=[VMEM] * 3,
        out_specs=(VMEM, VMEM),
        scratch_shapes=[pltpu.VMEM((2,) + stack.shape, BF16)],
        compiler_params=PARAMS,
        cost_estimate=cost(2**30, 2**19),
        name="near_frames",
    )(pair_frame, other_frame, entry_frame)


def near(pair_own, *rest):
    shape = pair_own.shape
    out = jax.ShapeDtypeStruct(shape, BF16)
    stack = stack_of(shape[0] // 2)
    return pl.pallas_call(
        near_kernel,
        out_shape=(out, out),
        in_specs=[VMEM] * (1 + len(rest)),
        out_specs=(VMEM, VMEM),
        scratch_shapes=[stack, stack],
        compiler_params=PARAMS,
        cost_estimate=cost(2**31, 2**19),
        name="near",
    )(pair_own, *rest)


def tick(moment, forward_index, backward_index, frames, *rest, earlier=None):
    channels, pixels = frames.shape[-2:]
    restored = jax.ShapeDtypeStruct((frames.shape[0], channels, pixels), BF16)
    state = jax.ShapeDtypeStruct((channels, pixels), BF16)
    operands = (forward_index, backward_index, frames, *rest)
    in_specs = [VMEM] * (3 + len(rest))
    aliases = {}
    if earlier is not None:
        aliases = {len(operands): 0}
        operands += (earlier,)
        in_specs.append(ANY)
    finals = (state, state) if moment > 0 else ()
    stack = stack_of(channels)
    return pl.pallas_call(
        functools.partial(tick_kernel, moment),
        out_shape=(restored,) + finals,
        in_specs=in_specs,
        out_specs=(ANY,) * (1 + len(finals)),
        scratch_shapes=[
            stack,
            stack,
            pltpu.VMEM((2, channels, pixels), BF16),
            pltpu.VMEM((channels, pixels), BF16),
            pltpu.SemaphoreType.DMA((2,)),
            pltpu.SemaphoreType.DMA((2,)),
        ],
        input_output_aliases=aliases,
        compiler_params=PARAMS,
        cost_estimate=cost(2**32, 2**19),
        name=f"tick_{moment}",
    )(*operands)


def sent(value, steps_even, steps_odd):
    count = lax.axis_size("tm")
    pairs = [(s, s + (steps_odd if s % 2 else steps_even)) for s in range(count)]
    return lax.ppermute(value, "tm", [(s, d) for s, d in pairs if 0 <= d < count])


def swapped(value):
    return lax.ppermute(value, "tile", [(0, 1), (1, 0)])


def later(value, *others):
    return lax.optimization_barrier((value, *others))[0]


def shards(
    frames,
    forward_carry,
    backward_carry,
    forward_source,
    backward_source,
    forward_entry,
    forward_blocks,
    backward_entry,
    backward_blocks,
    mixing_weight,
):
    payload = head(frames, forward_source, backward_source)
    pair_frame = sent(payload, 1, -1)
    near_state, far_state = pack(later(forward_carry, payload), backward_carry)
    pair_far = sent(far_state, -2, 2)
    other_far = sent(near_state, 2, -2)
    entry_frame, entry_warped, layers = pair_weights(
        later(forward_entry, near_state), forward_blocks, backward_entry, backward_blocks
    )
    parts = frame_parts(frames, later(entry_frame, pair_frame))
    other_frame = sent(pair_frame, 2, -2)
    pair_near = sent(later(near_state, pair_frame), 1, -1)
    other_near = sent(later(far_state, pair_frame), -1, 1)
    near_parts, lists = near_frames(pair_frame, other_frame, later(entry_frame, *parts))
    forward_one, backward_one = near(
        pair_far,
        swapped(later(pair_far, parts[0])),
        other_far,
        swapped(later(other_far, parts[0])),
        later(near_parts, pair_near),
        lists,
        entry_warped,
        layers,
    )
    restored, forward_final, backward_final = tick(
        1,
        forward_source,
        backward_source,
        frames,
        later(forward_one, other_near),
        swapped(forward_one),
        backward_one,
        swapped(backward_one),
        parts[1],
        entry_warped,
        layers,
        mixing_weight,
    )
    (restored,) = tick(
        0,
        forward_source,
        backward_source,
        frames,
        pair_near,
        swapped(pair_near),
        other_near,
        swapped(other_near),
        parts[0],
        entry_warped,
        layers,
        mixing_weight,
        earlier=restored,
    )
    return (restored[:, None, None], forward_final[None, None], backward_final[None, None])


def solution(mesh):
    placed = (
        P(None, ("groups", "tm"), "tile", None, None),
        P(("groups", "tm"), "tile", None, None),
        P(("groups", "tm"), "tile", None, None),
        P(None, ("groups", "tm"), "tile"),
        P(None, ("groups", "tm"), "tile"),
        P(),
        P(),
        P(),
        P(),
        P(),
    )
    return jax.shard_map(
        shards,
        mesh=mesh,
        in_specs=placed,
        out_specs=(
            P(None, ("groups", "tm"), "tile", None, None),
            P(("groups", "tm"), "tile", None, None),
            P(("groups", "tm"), "tile", None, None),
        ),
        check_vma=False,
    )
```

```python
import functools

import jax
import jax.numpy as jnp
from jax import lax
from jax.experimental import pallas as pl
from jax.experimental.pallas import tpu as pltpu
from jax.sharding import PartitionSpec as P

RH = 32
RW = 64
BH = 8
BW = 16
LANES = 128
BLOCK_ROWS = RH // BH
BLOCK_COLS = RW // BW
REGION_BLOCKS = BLOCK_ROWS * BLOCK_COLS
PAIRS = RW // 2
BLOCK_PAIRS = BW // 2
NATURAL = RH * RW // LANES
ROWS_IN_GROUP = LANES // RW
QUADS = BH // ROWS_IN_GROUP
BF16 = jnp.bfloat16
F32 = jnp.float32


def lanes(shape):
    return lax.broadcasted_iota(jnp.int32, shape, len(shape) - 1)


def cut(value, count):
    return [value[:, v * LANES : (v + 1) * LANES] for v in range(count)]


def one_hot(depth, target):
    row = lax.broadcasted_iota(jnp.int32, (depth, target.shape[1]), 0)
    return (row == target).astype(F32).astype(BF16)


def dot(a, b):
    return jnp.dot(a, b, preferred_element_type=F32)


def pairing():
    width = BLOCK_ROWS * LANES
    n = lanes((1, width))
    parity = n // LANES
    target = n % LANES // PAIRS * LANES + parity // 2 * RW + n % PAIRS * 2 + parity % 2
    return one_hot(width, target)


def to_paired(groups, matrix):
    channels = groups[0].shape[0]
    rows = [
        jnp.concatenate([groups[QUADS * br + j] for br in range(BLOCK_ROWS)], axis=1) for j in range(QUADS)
    ]
    moved = dot(jnp.concatenate(rows, axis=0), matrix).astype(BF16)
    out = []
    for j in range(QUADS):
        here = cut(moved[j * channels : (j + 1) * channels], BLOCK_ROWS)
        for q in range(ROWS_IN_GROUP):
            out.append(jnp.concatenate(here[2 * q : 2 * q + 2], axis=0))
    return out


def unpairing():
    width = BLOCK_ROWS * LANES
    n = lanes((1, width))
    column = n % RW
    target = (n % LANES // RW * 2 + column % 2) * LANES + n // LANES * PAIRS + column // 2
    return one_hot(width, target)


def to_natural(maps, matrix):
    channels = maps[0][0].shape[0] // 2
    rows = []
    for groups in maps:
        for j in range(QUADS):
            parts = []
            for q in range(ROWS_IN_GROUP):
                group = groups[ROWS_IN_GROUP * j + q]
                parts += [group[:channels], group[channels:]]
            rows.append(jnp.concatenate(parts, axis=1))
    moved = dot(jnp.concatenate(rows, axis=0), matrix).astype(BF16)
    out = []
    for m in range(len(maps)):
        here = [
            cut(moved[(m * QUADS + j) * channels : (m * QUADS + j + 1) * channels], BLOCK_ROWS)
            for j in range(QUADS)
        ]
        out.append([here[j][br] for br in range(BLOCK_ROWS) for j in range(QUADS)])
    return out


def lane_target(source, tile):
    slot = (source // REGION_BLOCKS + tile) % 2
    return slot * LANES + source % REGION_BLOCKS * BLOCK_PAIRS


def spread(index):
    row = lax.broadcasted_iota(jnp.int32, (REGION_BLOCKS, LANES), 0)
    places = (row == lanes((REGION_BLOCKS, LANES)) // BLOCK_PAIRS).astype(F32).astype(BF16)
    rows = jnp.broadcast_to(index.astype(F32), (REGION_BLOCKS, REGION_BLOCKS)).astype(BF16)
    return dot(rows, places)


def target_of(source, tile):
    return lane_target(source.astype(jnp.int32), tile) + lanes((1, LANES)) % BLOCK_PAIRS


def put_taps(stack, i, group):
    channels = group.shape[0] // 2
    shape = (channels, LANES)
    lane = lanes(shape)
    zero = jnp.zeros(shape, BF16)
    before = jnp.where(lane % PAIRS == 0, zero, pltpu.roll(group[channels:], 1, 1))
    after = jnp.where(lane % PAIRS == PAIRS - 1, zero, pltpu.roll(group[:channels], LANES - 1, 1))
    put_rows(stack, i, (before, group[:channels], group[channels:], after))


def put_rows(stack, i, parts):
    value = jnp.concatenate(parts, axis=0)
    stack[:, (i + 1) * LANES : (i + 2) * LANES] = value
    lane = lanes(value.shape)
    zero = jnp.zeros(value.shape, BF16)
    if i == BH - 1:
        stack[:, :LANES] = jnp.where(lane < PAIRS, zero, pltpu.roll(value, PAIRS, 1))
    if i == 0:
        below = pltpu.roll(value, LANES - PAIRS, 1)
        stack[:, (BH + 1) * LANES :] = jnp.where(lane >= LANES - PAIRS, zero, below)


def picks_of(target):
    lane = lanes((1, LANES))
    before = jnp.where(lane % PAIRS == 0, -1, pltpu.roll(target, 1, 1))
    after = jnp.where(lane % PAIRS == PAIRS - 1, -1, pltpu.roll(target, LANES - 1, 1))
    depth = 2 * LANES
    return (
        one_hot(depth, jnp.concatenate([target, after], axis=1)),
        one_hot(depth, jnp.concatenate([before, target], axis=1)),
    )


def put_warped(stack, tiles, picks):
    channels = tiles[0][0].shape[0] // 2
    moved = []
    for half in range(2):
        rows = slice(half * channels, (half + 1) * channels)
        wide = [jnp.concatenate([t[i][rows] for t in tiles], axis=1) for i in range(BH)]
        moved.append(dot(jnp.concatenate(wide, axis=0), picks[half]).astype(BF16))
    for i in range(BH):
        even, odd = [m[i * channels : (i + 1) * channels] for m in moved]
        put_rows(stack, i, (odd[:, :LANES], even[:, :LANES], odd[:, LANES:], even[:, LANES:]))


def convolve(stack, weight, start=None):
    for t in (2, 4, 0, 6):
        total = None if start is None else start[:, t * LANES : (t + 2) * LANES]
        for a in range(3):
            part = dot(weight[a], stack[:, (t + a) * LANES : (t + a + 2) * LANES])
            total = part if total is None else total + part
        yield t, total[:, :LANES]
        yield t + 1, total[:, LANES:]


def lrelu(u):
    return jnp.maximum(u, 0.1 * u).astype(BF16)


def both_convolve(stacks, weights, starts):
    for here in zip(*(convolve(*operands) for operands in zip(stacks, weights, starts))):
        yield here[0][0], [u for _, u in here]


def chains(first, second, entry, starts, layers):
    both = range(2)
    nothing = (None, None)
    hidden = [[None] * BH for _ in both]
    for i, values in both_convolve(first, [entry.at[d] for d in both], starts):
        for d in both:
            hidden[d][i] = lrelu(values[d])
            put_taps(second[d], i, hidden[d][i])
    for layer in range(layers.shape[1]):
        for i, values in both_convolve(second, [layers.at[d, layer, 0] for d in both], nothing):
            for d in both:
                put_taps(first[d], i, lrelu(values[d]))
        for i, values in both_convolve(first, [layers.at[d, layer, 1] for d in both], nothing):
            for d in both:
                hidden[d][i] = (hidden[d][i].astype(F32) + values[d]).astype(BF16)
                if layer + 1 < layers.shape[1]:
                    put_taps(second[d], i, hidden[d][i])
    return hidden


def even_segment():
    return lax.axis_index("tm") % 2 == 0


def head_kernel(frames, forward_index, backward_index, payload, index, sem, index_sems):
    channels, pixels = frames.shape[-2:]
    copies = [pltpu.make_async_copy(frames.at[0, 0, 0], payload.at[:, :pixels], sem)]
    for d, source in enumerate((forward_index, backward_index)):
        copies.append(pltpu.make_async_copy(source, index.at[d], index_sems.at[d]))
    for copy in copies:
        copy.start()
    half = channels // 2
    for d in range(2):
        copies[1 + d].wait()
        source = spread(index[d, 0]).astype(BF16)
        for row in range(d * half, (d + 1) * half, REGION_BLOCKS):
            payload[row : row + REGION_BLOCKS, pixels:] = source
    copies[0].wait()


def pack_kernel(forward, backward, near_out, far_out):
    matrix = pairing()
    even = even_segment()
    packed = [to_paired(cut(source[0, 0], NATURAL), matrix) for source in (forward, backward)]
    for i, (f, b) in enumerate(zip(*packed)):
        columns = slice(i * LANES, (i + 1) * LANES)
        near_out[:, columns] = jnp.where(even, f, b)
        far_out[:, columns] = jnp.where(even, b, f)


def frame_kernel(frames, entry_frame, matrix, *rest):
    paired, parts, stack = rest
    channels = frames.shape[-2]
    for moment in range(frames.shape[0]):
        for i, group in enumerate(to_paired(cut(frames[moment, 0, 0], NATURAL), matrix[...])):
            put_taps(stack, i, group)
            paired[moment, :, i * LANES : (i + 1) * LANES] = group
        for i, group in convolve(stack, entry_frame):
            for d in range(2):
                parts[moment, d, :, i * LANES : (i + 1) * LANES] = group[
                    2 * d * channels : 2 * (d + 1) * channels
                ]


def tap_weight(taps):
    zero = jnp.zeros_like(taps[0])
    return jnp.concatenate(
        [jnp.concatenate(taps + [zero], axis=1), jnp.concatenate([zero] + taps, axis=1)], axis=0
    )


def block_diagonal(weight):
    zero = jnp.zeros_like(weight)
    return jnp.concatenate(
        [jnp.concatenate([weight, zero], axis=1), jnp.concatenate([zero, weight], axis=1)], axis=0
    )


def weights_kernel(fe, fb, be, bb, mixing, entry_frame, entry_warped, layers, mix_pair, matrix, back):
    channels = fe.shape[1]
    matrix[...] = pairing()
    back[...] = unpairing()
    for d, (entry, blocks) in enumerate(((fe, fb), (be, bb))):
        mix_pair[d] = block_diagonal(mixing[:, d * channels : (d + 1) * channels])
        for a in range(3):
            taps = [entry[3 * a + b] for b in range(3)]
            entry_frame[a, 2 * d * channels : 2 * (d + 1) * channels] = tap_weight(
                [t[:, :channels] for t in taps]
            )
            entry_warped[d, a] = tap_weight([t[:, channels:] for t in taps])
            for layer in range(blocks.shape[0]):
                for part in range(2):
                    layers[d, layer, part, a] = tap_weight(
                        [blocks[layer, part, 3 * a + b] for b in range(3)]
                    )


def picks_kernel(forward_index, backward_index, out):
    tile = lax.axis_index("tile")
    for moment in range(out.shape[0]):
        for d, index in enumerate((forward_index, backward_index)):
            for half, pick in enumerate(picks_of(target_of(spread(index[moment])[:1], tile))):
                out[moment, d, half] = pick


def by_direction(even, pair_side, other_side):
    first, second = pair_side[...], other_side[...]
    return jnp.where(even, second, first), jnp.where(even, first, second)


def near_frame_kernel(pair_frame, other_frame, entry_frame, matrix, out, picks, stack):
    even = even_segment()
    tile = lax.axis_index("tile")
    width = NATURAL * LANES
    channels = pair_frame.shape[0]
    half = channels // 2
    payloads = by_direction(even, pair_frame, other_frame)
    for d in range(2):
        for i, group in enumerate(to_paired(cut(payloads[d][:, :width], NATURAL), matrix[...])):
            put_taps(stack.at[d], i, group)
        source = payloads[d][d * half : d * half + REGION_BLOCKS, width:].astype(F32)[:1]
        for part, pick in enumerate(picks_of(target_of(source, tile))):
            picks[d, part] = pick
    for d in range(2):
        weight = [entry_frame[a, 2 * d * channels : 2 * (d + 1) * channels] for a in range(3)]
        for i, group in convolve(stack.at[d], weight):
            out[d, :, i * LANES : (i + 1) * LANES] = group


def near_kernel(
    pair_own,
    pair_swapped,
    other_own,
    other_swapped,
    starts,
    picks,
    entry_warped,
    layers,
    forward_out,
    backward_out,
    *stacks,
):
    even = even_segment()
    firsts, seconds = stacks[:2], stacks[2:]
    owns = by_direction(even, pair_own, other_own)
    others = by_direction(even, pair_swapped, other_swapped)
    for d in range(2):
        put_warped(firsts[d], (cut(owns[d], BH), cut(others[d], BH)), picks[d])
    hidden = chains(firsts, seconds, entry_warped, [starts.at[d] for d in range(2)], layers)
    for groups, out in zip(hidden, (forward_out, backward_out)):
        for i, group in enumerate(groups):
            out[:, i * LANES : (i + 1) * LANES] = group


def mix(weight, state, total):
    out = []
    for i in range(0, BH, 2):
        wide = dot(weight, jnp.concatenate(state[i : i + 2], axis=1))
        out += [total[i] + wide[:, :LANES], total[i + 1] + wide[:, LANES:]]
    return out


def rounded(groups):
    return [u.astype(BF16) for u in groups]


def put_natural(out, groups):
    for v, group in enumerate(groups):
        out[:, v * LANES : (v + 1) * LANES] = group


def tick_kernel(
    moment,
    first_own,
    first_swapped,
    second_own,
    second_swapped,
    picks,
    paired,
    parts,
    entry_warped,
    layers,
    mix_pair,
    back,
    *rest,
):
    *_, restored, forward_final, backward_final = rest[:-8] if moment > 0 else rest[:-8] + (None, None)
    *stacks, finals, mixed, final_sems, mixed_sem = rest[-8:]
    firsts, seconds = stacks[:2], stacks[2:]
    owns, others = (first_own[...], second_own[...]), (first_swapped[...], second_swapped[...])
    if moment == 0:
        even = even_segment()
        owns = by_direction(even, first_own, second_own)
        others = by_direction(even, first_swapped, second_swapped)
    for d in range(2):
        put_warped(firsts[d], (cut(owns[d], BH), cut(others[d], BH)), picks[moment, d])
    hidden = chains(firsts, seconds, entry_warped, [parts.at[moment, d] for d in range(2)], layers)
    total = cut(paired[moment].astype(F32), BH)
    for d in range(2):
        total = mix(mix_pair[d], hidden[d], total)
    natural = to_natural([rounded(total)] + (hidden if moment > 0 else []), back[...])
    put_natural(mixed, natural[0])
    copies = [pltpu.make_async_copy(mixed, restored.at[moment], mixed_sem)]
    copies[0].start()
    for d, groups in enumerate(natural[1:]):
        put_natural(finals.at[d], groups)
        out = (forward_final, backward_final)[d]
        copies.append(pltpu.make_async_copy(finals.at[d], out, final_sems.at[d]))
        copies[-1].start()
    for copy in copies:
        copy.wait()


VMEM = pl.BlockSpec(memory_space=pltpu.VMEM)
ANY = pl.BlockSpec(memory_space=pl.ANY)
PARAMS = pltpu.CompilerParams(vmem_limit_bytes=32 * 2**20)


def cost(flops, count):
    return pl.CostEstimate(flops=flops, bytes_accessed=count, transcendentals=0)


def head(frames, forward_source, backward_source):
    channels, pixels = frames.shape[-2:]
    return pl.pallas_call(
        head_kernel,
        out_shape=jax.ShapeDtypeStruct((channels, pixels + LANES), BF16),
        in_specs=[ANY] * 3,
        out_specs=VMEM,
        scratch_shapes=[
            pltpu.VMEM((2,) + forward_source.shape, jnp.int32),
            pltpu.SemaphoreType.DMA,
            pltpu.SemaphoreType.DMA((2,)),
        ],
        compiler_params=pltpu.CompilerParams(vmem_limit_bytes=62 * 2**20),
        cost_estimate=cost(2**30, 2**19),
        name="head",
    )(frames, forward_source, backward_source)


def pack(forward, backward):
    channels, pixels = forward.shape[-2:]
    shape = jax.ShapeDtypeStruct((2 * channels, pixels // 2), BF16)
    return pl.pallas_call(
        pack_kernel,
        out_shape=(shape, shape),
        in_specs=[VMEM] * 2,
        out_specs=(VMEM, VMEM),
        compiler_params=PARAMS,
        cost_estimate=cost(2**29, 2**19),
        name="pack",
    )(forward, backward)


def pair_weights(forward_entry, forward_blocks, backward_entry, backward_blocks, mixing):
    channels = forward_entry.shape[1]
    count = forward_blocks.shape[0]
    tall, wide, square = 2 * channels, 4 * channels, BLOCK_ROWS * LANES
    shapes = (
        (3, wide, wide),
        (2, 3, tall, wide),
        (2, count, 2, 3, tall, wide),
        (2, tall, tall),
        (square, square),
        (square, square),
    )
    return pl.pallas_call(
        weights_kernel,
        out_shape=tuple(jax.ShapeDtypeStruct(shape, BF16) for shape in shapes),
        in_specs=[VMEM] * 5,
        out_specs=(VMEM,) * len(shapes),
        compiler_params=PARAMS,
        cost_estimate=cost(2**29, 2**20),
        name="pair_weights",
    )(forward_entry, forward_blocks, backward_entry, backward_blocks, mixing)


def all_picks(forward_source, backward_source):
    return pl.pallas_call(
        picks_kernel,
        out_shape=jax.ShapeDtypeStruct((forward_source.shape[0], 2, 2, 2 * LANES, 2 * LANES), BF16),
        in_specs=[VMEM] * 2,
        out_specs=VMEM,
        compiler_params=PARAMS,
        cost_estimate=cost(2**29, 2**20),
        name="all_picks",
    )(forward_source, backward_source)


def stack_of(channels):
    return pltpu.VMEM((4 * channels, (BH + 2) * LANES), BF16)


def paired_shape(frames):
    channels, pixels = frames.shape[-2:]
    return (2 * channels, pixels // 2)


def frame_parts(frames, entry_frame, matrix):
    moments = frames.shape[0]
    paired = paired_shape(frames)
    return pl.pallas_call(
        frame_kernel,
        out_shape=(
            jax.ShapeDtypeStruct((moments,) + paired, BF16),
            jax.ShapeDtypeStruct((moments, 2) + paired, F32),
        ),
        in_specs=[VMEM] * 3,
        out_specs=(VMEM, VMEM),
        scratch_shapes=[stack_of(frames.shape[-2])],
        compiler_params=PARAMS,
        cost_estimate=cost(2**31, 2**20),
        name="frame_parts",
    )(frames, entry_frame, matrix)


def near_frames(pair_frame, other_frame, entry_frame, matrix):
    channels, width = pair_frame.shape
    stack = stack_of(channels)
    return pl.pallas_call(
        near_frame_kernel,
        out_shape=(
            jax.ShapeDtypeStruct((2, 2 * channels, (width - LANES) // 2), F32),
            jax.ShapeDtypeStruct((2, 2, 2 * LANES, 2 * LANES), BF16),
        ),
        in_specs=[VMEM] * 4,
        out_specs=(VMEM, VMEM),
        scratch_shapes=[pltpu.VMEM((2,) + stack.shape, BF16)],
        compiler_params=PARAMS,
        cost_estimate=cost(2**30, 2**19),
        name="near_frames",
    )(pair_frame, other_frame, entry_frame, matrix)


def near(pair_own, *rest):
    shape = pair_own.shape
    out = jax.ShapeDtypeStruct(shape, BF16)
    stack = stack_of(shape[0] // 2)
    return pl.pallas_call(
        near_kernel,
        out_shape=(out, out),
        in_specs=[VMEM] * (1 + len(rest)),
        out_specs=(VMEM, VMEM),
        scratch_shapes=[stack] * 4,
        compiler_params=PARAMS,
        cost_estimate=cost(2**31, 2**19),
        name="near",
    )(pair_own, *rest)


def tick(moment, frames, *operands, earlier=None):
    channels, pixels = frames.shape[-2:]
    restored = jax.ShapeDtypeStruct((frames.shape[0], channels, pixels), BF16)
    state = jax.ShapeDtypeStruct((channels, pixels), BF16)
    in_specs = [VMEM] * len(operands)
    aliases = {}
    if earlier is not None:
        aliases = {len(operands): 0}
        operands += (earlier,)
        in_specs.append(ANY)
    finals = (state, state) if moment > 0 else ()
    stack = stack_of(channels)
    return pl.pallas_call(
        functools.partial(tick_kernel, moment),
        out_shape=(restored,) + finals,
        in_specs=in_specs,
        out_specs=(ANY,) * (1 + len(finals)),
        scratch_shapes=[
            *[stack] * 4,
            pltpu.VMEM((2, channels, pixels), BF16),
            pltpu.VMEM((channels, pixels), BF16),
            pltpu.SemaphoreType.DMA((2,)),
            pltpu.SemaphoreType.DMA,
        ],
        input_output_aliases=aliases,
        compiler_params=PARAMS,
        cost_estimate=cost(2**32, 2**19),
        name=f"tick_{moment}",
    )(*operands)


def sent(value, steps_even, steps_odd):
    count = lax.axis_size("tm")
    pairs = [(s, s + (steps_odd if s % 2 else steps_even)) for s in range(count)]
    return lax.ppermute(value, "tm", [(s, d) for s, d in pairs if 0 <= d < count])


def swapped(value):
    return lax.ppermute(value, "tile", [(0, 1), (1, 0)])


def later(value, *others):
    return lax.optimization_barrier((value, *others))[0]


def shards(
    frames,
    forward_carry,
    backward_carry,
    forward_source,
    backward_source,
    forward_entry,
    forward_blocks,
    backward_entry,
    backward_blocks,
    mixing_weight,
):
    payload = head(frames, forward_source, backward_source)
    pair_frame = sent(payload, 1, -1)
    near_state, far_state = pack(later(forward_carry, payload), backward_carry)
    pair_far = sent(far_state, -2, 2)
    other_far = sent(near_state, 2, -2)
    entry_frame, entry_warped, layers, mix_pair, matrix, back = pair_weights(
        later(forward_entry, near_state), forward_blocks, backward_entry, backward_blocks, mixing_weight
    )
    picks = all_picks(forward_source, backward_source)
    paired, parts = frame_parts(frames, later(entry_frame, pair_frame), matrix)
    other_frame = sent(pair_frame, 2, -2)
    pair_near = sent(later(near_state, pair_frame), 1, -1)
    other_near = sent(later(far_state, pair_frame), -1, 1)
    near_parts, near_picks = near_frames(pair_frame, other_frame, later(entry_frame, parts, picks), matrix)
    forward_one, backward_one = near(
        pair_far,
        swapped(later(pair_far, parts)),
        other_far,
        swapped(later(other_far, parts)),
        later(near_parts, pair_near, other_near),
        near_picks,
        entry_warped,
        layers,
    )
    tables = (picks, paired, parts, entry_warped, layers, mix_pair, back)
    (restored,) = tick(
        0, frames, pair_near, swapped(pair_near), other_near, swapped(other_near), *tables
    )
    restored, forward_final, backward_final = tick(
        1,
        frames,
        forward_one,
        swapped(forward_one),
        backward_one,
        swapped(backward_one),
        *tables,
        earlier=restored,
    )
    return (restored[:, None, None], forward_final[None, None], backward_final[None, None])


def solution(mesh):
    placed = (
        P(None, ("groups", "tm"), "tile", None, None),
        P(("groups", "tm"), "tile", None, None),
        P(("groups", "tm"), "tile", None, None),
        P(None, ("groups", "tm"), "tile"),
        P(None, ("groups", "tm"), "tile"),
        P(),
        P(),
        P(),
        P(),
        P(),
    )
    return jax.shard_map(
        shards,
        mesh=mesh,
        in_specs=placed,
        out_specs=(
            P(None, ("groups", "tm"), "tile", None, None),
            P(("groups", "tm"), "tile", None, None),
            P(("groups", "tm"), "tile", None, None),
        ),
        check_vma=False,
    )
```

```python
import functools

import jax
import jax.numpy as jnp
from jax import lax
from jax.experimental import pallas as pl
from jax.experimental.pallas import tpu as pltpu
from jax.sharding import PartitionSpec as P

RH = 32
RW = 64
BH = 8
BW = 16
LANES = 128
BLOCK_ROWS = RH // BH
BLOCK_COLS = RW // BW
REGION_BLOCKS = BLOCK_ROWS * BLOCK_COLS
PAIRS = RW // 2
BLOCK_PAIRS = BW // 2
NATURAL = RH * RW // LANES
ROWS_IN_GROUP = LANES // RW
QUADS = BH // ROWS_IN_GROUP
BF16 = jnp.bfloat16
F32 = jnp.float32


def lanes(shape):
    return lax.broadcasted_iota(jnp.int32, shape, len(shape) - 1)


def cut(value, count):
    return [value[:, v * LANES : (v + 1) * LANES] for v in range(count)]


def one_hot(depth, target):
    row = lax.broadcasted_iota(jnp.int32, (depth, target.shape[1]), 0)
    return (row == target).astype(F32).astype(BF16)


def dot(a, b):
    return jnp.dot(a, b, preferred_element_type=F32)


def pairing():
    width = BLOCK_ROWS * LANES
    n = lanes((1, width))
    parity = n // LANES
    target = n % LANES // PAIRS * LANES + parity // 2 * RW + n % PAIRS * 2 + parity % 2
    return one_hot(width, target)


def to_paired(groups, matrix):
    channels = groups[0].shape[0]
    rows = [
        jnp.concatenate([groups[QUADS * br + j] for br in range(BLOCK_ROWS)], axis=1) for j in range(QUADS)
    ]
    moved = dot(jnp.concatenate(rows, axis=0), matrix).astype(BF16)
    out = []
    for j in range(QUADS):
        here = cut(moved[j * channels : (j + 1) * channels], BLOCK_ROWS)
        for q in range(ROWS_IN_GROUP):
            out.append(jnp.concatenate(here[2 * q : 2 * q + 2], axis=0))
    return out


def unpairing():
    width = BLOCK_ROWS * LANES
    n = lanes((1, width))
    column = n % RW
    target = (n % LANES // RW * 2 + column % 2) * LANES + n // LANES * PAIRS + column // 2
    return one_hot(width, target)


def to_natural(maps, matrix):
    channels = maps[0][0].shape[0] // 2
    rows = []
    for groups in maps:
        for j in range(QUADS):
            parts = []
            for q in range(ROWS_IN_GROUP):
                group = groups[ROWS_IN_GROUP * j + q]
                parts += [group[:channels], group[channels:]]
            rows.append(jnp.concatenate(parts, axis=1))
    moved = dot(jnp.concatenate(rows, axis=0), matrix).astype(BF16)
    out = []
    for m in range(len(maps)):
        here = [
            cut(moved[(m * QUADS + j) * channels : (m * QUADS + j + 1) * channels], BLOCK_ROWS)
            for j in range(QUADS)
        ]
        out.append([here[j][br] for br in range(BLOCK_ROWS) for j in range(QUADS)])
    return out


def lane_target(source, tile):
    slot = (source // REGION_BLOCKS + tile) % 2
    return slot * LANES + source % REGION_BLOCKS * BLOCK_PAIRS


def spread(index):
    row = lax.broadcasted_iota(jnp.int32, (REGION_BLOCKS, LANES), 0)
    places = (row == lanes((REGION_BLOCKS, LANES)) // BLOCK_PAIRS).astype(F32).astype(BF16)
    rows = jnp.broadcast_to(index.astype(F32), (REGION_BLOCKS, REGION_BLOCKS)).astype(BF16)
    return dot(rows, places)


def target_of(source, tile):
    return lane_target(source.astype(jnp.int32), tile) + lanes((1, LANES)) % BLOCK_PAIRS


def put_taps(stack, i, group):
    channels = group.shape[0] // 2
    shape = (channels, LANES)
    lane = lanes(shape)
    zero = jnp.zeros(shape, BF16)
    before = jnp.where(lane % PAIRS == 0, zero, pltpu.roll(group[channels:], 1, 1))
    after = jnp.where(lane % PAIRS == PAIRS - 1, zero, pltpu.roll(group[:channels], LANES - 1, 1))
    put_rows(stack, i, (before, group[:channels], group[channels:], after))


def put_rows(stack, i, parts):
    value = jnp.concatenate(parts, axis=0)
    stack[:, (i + 1) * LANES : (i + 2) * LANES] = value
    lane = lanes(value.shape)
    zero = jnp.zeros(value.shape, BF16)
    if i == BH - 1:
        stack[:, :LANES] = jnp.where(lane < PAIRS, zero, pltpu.roll(value, PAIRS, 1))
    if i == 0:
        below = pltpu.roll(value, LANES - PAIRS, 1)
        stack[:, (BH + 1) * LANES :] = jnp.where(lane >= LANES - PAIRS, zero, below)


def picks_of(target):
    lane = lanes((1, LANES))
    before = jnp.where(lane % PAIRS == 0, -1, pltpu.roll(target, 1, 1))
    after = jnp.where(lane % PAIRS == PAIRS - 1, -1, pltpu.roll(target, LANES - 1, 1))
    depth = 2 * LANES
    return (
        one_hot(depth, jnp.concatenate([target, after], axis=1)),
        one_hot(depth, jnp.concatenate([before, target], axis=1)),
    )


def put_warped(stack, tiles, picks):
    channels = tiles[0][0].shape[0] // 2
    moved = []
    for half in range(2):
        rows = slice(half * channels, (half + 1) * channels)
        wide = [jnp.concatenate([t[i][rows] for t in tiles], axis=1) for i in range(BH)]
        moved.append(dot(jnp.concatenate(wide, axis=0), picks[half]).astype(BF16))
    for i in range(BH):
        even, odd = [m[i * channels : (i + 1) * channels] for m in moved]
        put_rows(stack, i, (odd[:, :LANES], even[:, :LANES], odd[:, LANES:], even[:, LANES:]))


def convolve(stack, weight, start=None):
    for t in (2, 4, 0, 6):
        total = None if start is None else start[:, t * LANES : (t + 2) * LANES]
        for a in range(3):
            part = dot(weight[a], stack[:, (t + a) * LANES : (t + a + 2) * LANES])
            total = part if total is None else total + part
        yield t, total[:, :LANES]
        yield t + 1, total[:, LANES:]


def lrelu(u):
    return jnp.maximum(u, 0.1 * u).astype(BF16)


def both_convolve(stacks, weights, starts):
    for here in zip(*(convolve(*operands) for operands in zip(stacks, weights, starts))):
        yield here[0][0], [u for _, u in here]


def chains(first, second, entry, starts, layers):
    both = range(2)
    nothing = (None, None)
    hidden = [[None] * BH for _ in both]
    for i, values in both_convolve(first, [entry.at[d] for d in both], starts):
        for d in both:
            hidden[d][i] = lrelu(values[d])
            put_taps(second[d], i, hidden[d][i])
    for layer in range(layers.shape[1]):
        for i, values in both_convolve(second, [layers.at[d, layer, 0] for d in both], nothing):
            for d in both:
                put_taps(first[d], i, lrelu(values[d]))
        for i, values in both_convolve(first, [layers.at[d, layer, 1] for d in both], nothing):
            for d in both:
                hidden[d][i] = (hidden[d][i].astype(F32) + values[d]).astype(BF16)
                if layer + 1 < layers.shape[1]:
                    put_taps(second[d], i, hidden[d][i])
    return hidden


def even_segment():
    return lax.axis_index("tm") % 2 == 0


def head_kernel(frames, forward_index, backward_index, payload, index, sem, index_sems):
    channels, pixels = frames.shape[-2:]
    copies = [pltpu.make_async_copy(frames.at[0, 0, 0], payload.at[:, :pixels], sem)]
    for d, source in enumerate((forward_index, backward_index)):
        copies.append(pltpu.make_async_copy(source, index.at[d], index_sems.at[d]))
    for copy in copies:
        copy.start()
    half = channels // 2
    for d in range(2):
        copies[1 + d].wait()
        source = spread(index[d, 0]).astype(BF16)
        for row in range(d * half, (d + 1) * half, REGION_BLOCKS):
            payload[row : row + REGION_BLOCKS, pixels:] = source
    copies[0].wait()


def pack_kernel(forward, backward, near_out, far_out):
    matrix = pairing()
    even = even_segment()
    packed = [to_paired(cut(source[0, 0], NATURAL), matrix) for source in (forward, backward)]
    for i, (f, b) in enumerate(zip(*packed)):
        columns = slice(i * LANES, (i + 1) * LANES)
        near_out[:, columns] = jnp.where(even, f, b)
        far_out[:, columns] = jnp.where(even, b, f)


def frame_kernel(frames, entry_frame, matrix, *rest):
    paired, parts, stack = rest
    channels = frames.shape[-2]
    for moment in range(frames.shape[0]):
        for i, group in enumerate(to_paired(cut(frames[moment, 0, 0], NATURAL), matrix[...])):
            put_taps(stack, i, group)
            paired[moment, :, i * LANES : (i + 1) * LANES] = group
        for i, group in convolve(stack, entry_frame):
            for d in range(2):
                parts[moment, d, :, i * LANES : (i + 1) * LANES] = group[
                    2 * d * channels : 2 * (d + 1) * channels
                ]


def tap_weight(taps):
    zero = jnp.zeros_like(taps[0])
    return jnp.concatenate(
        [jnp.concatenate(taps + [zero], axis=1), jnp.concatenate([zero] + taps, axis=1)], axis=0
    )


def block_diagonal(weight):
    zero = jnp.zeros_like(weight)
    return jnp.concatenate(
        [jnp.concatenate([weight, zero], axis=1), jnp.concatenate([zero, weight], axis=1)], axis=0
    )


def weights_kernel(fe, fb, be, bb, mixing, entry_frame, entry_warped, layers, mix_pair, matrix, back):
    channels = fe.shape[1]
    matrix[...] = pairing()
    back[...] = unpairing()
    for d, (entry, blocks) in enumerate(((fe, fb), (be, bb))):
        mix_pair[d] = block_diagonal(mixing[:, d * channels : (d + 1) * channels])
        for a in range(3):
            taps = [entry[3 * a + b] for b in range(3)]
            entry_frame[a, 2 * d * channels : 2 * (d + 1) * channels] = tap_weight(
                [t[:, :channels] for t in taps]
            )
            entry_warped[d, a] = tap_weight([t[:, channels:] for t in taps])
            for layer in range(blocks.shape[0]):
                for part in range(2):
                    layers[d, layer, part, a] = tap_weight(
                        [blocks[layer, part, 3 * a + b] for b in range(3)]
                    )


def picks_kernel(forward_index, backward_index, out):
    tile = lax.axis_index("tile")
    for moment in range(out.shape[0]):
        for d, index in enumerate((forward_index, backward_index)):
            for half, pick in enumerate(picks_of(target_of(spread(index[moment])[:1], tile))):
                out[moment, d, half] = pick


def by_direction(even, pair_side, other_side):
    first, second = pair_side[...], other_side[...]
    return jnp.where(even, second, first), jnp.where(even, first, second)


def near_frame_kernel(pair_frame, other_frame, entry_frame, matrix, out, picks, stack):
    even = even_segment()
    tile = lax.axis_index("tile")
    width = NATURAL * LANES
    channels = pair_frame.shape[0]
    half = channels // 2
    payloads = by_direction(even, pair_frame, other_frame)
    for d in range(2):
        for i, group in enumerate(to_paired(cut(payloads[d][:, :width], NATURAL), matrix[...])):
            put_taps(stack.at[d], i, group)
        source = payloads[d][d * half : d * half + REGION_BLOCKS, width:].astype(F32)[:1]
        for part, pick in enumerate(picks_of(target_of(source, tile))):
            picks[d, part] = pick
    for d in range(2):
        weight = [entry_frame[a, 2 * d * channels : 2 * (d + 1) * channels] for a in range(3)]
        for i, group in convolve(stack.at[d], weight):
            out[d, :, i * LANES : (i + 1) * LANES] = group


def near_kernel(
    pair_own,
    pair_swapped,
    other_own,
    other_swapped,
    starts,
    picks,
    entry_warped,
    layers,
    forward_out,
    backward_out,
    *stacks,
):
    even = even_segment()
    firsts, seconds = stacks[:2], stacks[2:]
    owns = by_direction(even, pair_own, other_own)
    others = by_direction(even, pair_swapped, other_swapped)
    for d in range(2):
        put_warped(firsts[d], (cut(owns[d], BH), cut(others[d], BH)), picks[d])
    hidden = chains(firsts, seconds, entry_warped, [starts.at[d] for d in range(2)], layers)
    for groups, out in zip(hidden, (forward_out, backward_out)):
        for i, group in enumerate(groups):
            out[:, i * LANES : (i + 1) * LANES] = group


def mix(weight, state, total):
    out = []
    for i in range(0, BH, 2):
        wide = dot(weight, jnp.concatenate(state[i : i + 2], axis=1))
        out += [total[i] + wide[:, :LANES], total[i + 1] + wide[:, LANES:]]
    return out


def rounded(groups):
    return [u.astype(BF16) for u in groups]


def put_natural(out, groups):
    for v, group in enumerate(groups):
        out[:, v * LANES : (v + 1) * LANES] = group


def tick_kernel(
    moment,
    first_own,
    first_swapped,
    second_own,
    second_swapped,
    picks,
    paired,
    parts,
    entry_warped,
    layers,
    mix_pair,
    back,
    *rest,
):
    *_, restored, forward_final, backward_final = rest[:-8] if moment > 0 else rest[:-8] + (None, None)
    *stacks, finals, mixed, final_sems, mixed_sem = rest[-8:]
    firsts, seconds = stacks[:2], stacks[2:]
    owns, others = (first_own[...], second_own[...]), (first_swapped[...], second_swapped[...])
    if moment == 0:
        even = even_segment()
        owns = by_direction(even, first_own, second_own)
        others = by_direction(even, first_swapped, second_swapped)
    for d in range(2):
        put_warped(firsts[d], (cut(owns[d], BH), cut(others[d], BH)), picks[moment, d])
    hidden = chains(firsts, seconds, entry_warped, [parts.at[moment, d] for d in range(2)], layers)
    copies = []
    for d, groups in enumerate(to_natural(hidden, back[...]) if moment > 0 else []):
        put_natural(finals.at[d], groups)
        out = (forward_final, backward_final)[d]
        copies.append(pltpu.make_async_copy(finals.at[d], out, final_sems.at[d]))
        copies[-1].start()
    total = cut(paired[moment].astype(F32), BH)
    for d in range(2):
        total = mix(mix_pair[d], hidden[d], total)
    put_natural(mixed, to_natural([rounded(total)], back[...])[0])
    copies.append(pltpu.make_async_copy(mixed, restored.at[moment], mixed_sem))
    copies[-1].start()
    for copy in copies:
        copy.wait()


VMEM = pl.BlockSpec(memory_space=pltpu.VMEM)
ANY = pl.BlockSpec(memory_space=pl.ANY)
PARAMS = pltpu.CompilerParams(vmem_limit_bytes=32 * 2**20)


def cost(flops, count):
    return pl.CostEstimate(flops=flops, bytes_accessed=count, transcendentals=0)


def head(frames, forward_source, backward_source):
    channels, pixels = frames.shape[-2:]
    return pl.pallas_call(
        head_kernel,
        out_shape=jax.ShapeDtypeStruct((channels, pixels + LANES), BF16),
        in_specs=[ANY] * 3,
        out_specs=VMEM,
        scratch_shapes=[
            pltpu.VMEM((2,) + forward_source.shape, jnp.int32),
            pltpu.SemaphoreType.DMA,
            pltpu.SemaphoreType.DMA((2,)),
        ],
        compiler_params=pltpu.CompilerParams(vmem_limit_bytes=62 * 2**20),
        cost_estimate=cost(2**30, 2**19),
        name="head",
    )(frames, forward_source, backward_source)


def pack(forward, backward):
    channels, pixels = forward.shape[-2:]
    shape = jax.ShapeDtypeStruct((2 * channels, pixels // 2), BF16)
    return pl.pallas_call(
        pack_kernel,
        out_shape=(shape, shape),
        in_specs=[VMEM] * 2,
        out_specs=(VMEM, VMEM),
        compiler_params=PARAMS,
        cost_estimate=cost(2**29, 2**19),
        name="pack",
    )(forward, backward)


def pair_weights(forward_entry, forward_blocks, backward_entry, backward_blocks, mixing):
    channels = forward_entry.shape[1]
    count = forward_blocks.shape[0]
    tall, wide, square = 2 * channels, 4 * channels, BLOCK_ROWS * LANES
    shapes = (
        (3, wide, wide),
        (2, 3, tall, wide),
        (2, count, 2, 3, tall, wide),
        (2, tall, tall),
        (square, square),
        (square, square),
    )
    return pl.pallas_call(
        weights_kernel,
        out_shape=tuple(jax.ShapeDtypeStruct(shape, BF16) for shape in shapes),
        in_specs=[VMEM] * 5,
        out_specs=(VMEM,) * len(shapes),
        compiler_params=PARAMS,
        cost_estimate=cost(2**29, 2**20),
        name="pair_weights",
    )(forward_entry, forward_blocks, backward_entry, backward_blocks, mixing)


def all_picks(forward_source, backward_source):
    return pl.pallas_call(
        picks_kernel,
        out_shape=jax.ShapeDtypeStruct((forward_source.shape[0], 2, 2, 2 * LANES, 2 * LANES), BF16),
        in_specs=[VMEM] * 2,
        out_specs=VMEM,
        compiler_params=PARAMS,
        cost_estimate=cost(2**29, 2**20),
        name="all_picks",
    )(forward_source, backward_source)


def stack_of(channels):
    return pltpu.VMEM((4 * channels, (BH + 2) * LANES), BF16)


def paired_shape(frames):
    channels, pixels = frames.shape[-2:]
    return (2 * channels, pixels // 2)


def frame_parts(frames, entry_frame, matrix):
    moments = frames.shape[0]
    paired = paired_shape(frames)
    return pl.pallas_call(
        frame_kernel,
        out_shape=(
            jax.ShapeDtypeStruct((moments,) + paired, BF16),
            jax.ShapeDtypeStruct((moments, 2) + paired, F32),
        ),
        in_specs=[VMEM] * 3,
        out_specs=(VMEM, VMEM),
        scratch_shapes=[stack_of(frames.shape[-2])],
        compiler_params=PARAMS,
        cost_estimate=cost(2**31, 2**20),
        name="frame_parts",
    )(frames, entry_frame, matrix)


def near_frames(pair_frame, other_frame, entry_frame, matrix):
    channels, width = pair_frame.shape
    stack = stack_of(channels)
    return pl.pallas_call(
        near_frame_kernel,
        out_shape=(
            jax.ShapeDtypeStruct((2, 2 * channels, (width - LANES) // 2), F32),
            jax.ShapeDtypeStruct((2, 2, 2 * LANES, 2 * LANES), BF16),
        ),
        in_specs=[VMEM] * 4,
        out_specs=(VMEM, VMEM),
        scratch_shapes=[pltpu.VMEM((2,) + stack.shape, BF16)],
        compiler_params=PARAMS,
        cost_estimate=cost(2**30, 2**19),
        name="near_frames",
    )(pair_frame, other_frame, entry_frame, matrix)


def near(pair_own, *rest):
    shape = pair_own.shape
    out = jax.ShapeDtypeStruct(shape, BF16)
    stack = stack_of(shape[0] // 2)
    return pl.pallas_call(
        near_kernel,
        out_shape=(out, out),
        in_specs=[VMEM] * (1 + len(rest)),
        out_specs=(VMEM, VMEM),
        scratch_shapes=[stack] * 4,
        compiler_params=PARAMS,
        cost_estimate=cost(2**31, 2**19),
        name="near",
    )(pair_own, *rest)


def tick(moment, frames, *operands, earlier=None):
    channels, pixels = frames.shape[-2:]
    restored = jax.ShapeDtypeStruct((frames.shape[0], channels, pixels), BF16)
    state = jax.ShapeDtypeStruct((channels, pixels), BF16)
    in_specs = [VMEM] * len(operands)
    aliases = {}
    if earlier is not None:
        aliases = {len(operands): 0}
        operands += (earlier,)
        in_specs.append(ANY)
    finals = (state, state) if moment > 0 else ()
    stack = stack_of(channels)
    return pl.pallas_call(
        functools.partial(tick_kernel, moment),
        out_shape=(restored,) + finals,
        in_specs=in_specs,
        out_specs=(ANY,) * (1 + len(finals)),
        scratch_shapes=[
            *[stack] * 4,
            pltpu.VMEM((2, channels, pixels), BF16),
            pltpu.VMEM((channels, pixels), BF16),
            pltpu.SemaphoreType.DMA((2,)),
            pltpu.SemaphoreType.DMA,
        ],
        input_output_aliases=aliases,
        compiler_params=PARAMS,
        cost_estimate=cost(2**32, 2**19),
        name=f"tick_{moment}",
    )(*operands)


def sent(value, steps_even, steps_odd):
    count = lax.axis_size("tm")
    pairs = [(s, s + (steps_odd if s % 2 else steps_even)) for s in range(count)]
    return lax.ppermute(value, "tm", [(s, d) for s, d in pairs if 0 <= d < count])


def swapped(value):
    return lax.ppermute(value, "tile", [(0, 1), (1, 0)])


def later(value, *others):
    return lax.optimization_barrier((value, *others))[0]


def shards(
    frames,
    forward_carry,
    backward_carry,
    forward_source,
    backward_source,
    forward_entry,
    forward_blocks,
    backward_entry,
    backward_blocks,
    mixing_weight,
):
    payload = head(frames, forward_source, backward_source)
    pair_frame = sent(payload, 1, -1)
    near_state, far_state = pack(later(forward_carry, payload), backward_carry)
    pair_far = sent(far_state, -2, 2)
    other_far = sent(near_state, 2, -2)
    entry_frame, entry_warped, layers, mix_pair, matrix, back = pair_weights(
        later(forward_entry, near_state), forward_blocks, backward_entry, backward_blocks, mixing_weight
    )
    picks = all_picks(forward_source, backward_source)
    paired, parts = frame_parts(frames, later(entry_frame, pair_frame), matrix)
    other_frame = sent(pair_frame, 2, -2)
    pair_near = sent(near_state, 1, -1)
    other_near = sent(later(far_state, pair_frame), -1, 1)
    near_parts, near_picks = near_frames(pair_frame, other_frame, later(entry_frame, parts, picks), matrix)
    forward_one, backward_one = near(
        pair_far,
        swapped(later(pair_far, parts)),
        other_far,
        swapped(later(other_far, parts)),
        later(near_parts, pair_near, other_near),
        near_picks,
        entry_warped,
        layers,
    )
    tables = (picks, paired, parts, entry_warped, layers, mix_pair, back)
    (restored,) = tick(
        0, frames, pair_near, swapped(pair_near), other_near, swapped(other_near), *tables
    )
    restored, forward_final, backward_final = tick(
        1,
        frames,
        forward_one,
        swapped(forward_one),
        backward_one,
        swapped(backward_one),
        *tables,
        earlier=restored,
    )
    return (restored[:, None, None], forward_final[None, None], backward_final[None, None])


def solution(mesh):
    placed = (
        P(None, ("groups", "tm"), "tile", None, None),
        P(("groups", "tm"), "tile", None, None),
        P(("groups", "tm"), "tile", None, None),
        P(None, ("groups", "tm"), "tile"),
        P(None, ("groups", "tm"), "tile"),
        P(),
        P(),
        P(),
        P(),
        P(),
    )
    return jax.shard_map(
        shards,
        mesh=mesh,
        in_specs=placed,
        out_specs=(
            P(None, ("groups", "tm"), "tile", None, None),
            P(("groups", "tm"), "tile", None, None),
            P(("groups", "tm"), "tile", None, None),
        ),
        check_vma=False,
    )
```

```python
import functools

import jax
import jax.numpy as jnp
from jax import lax
from jax.experimental import pallas as pl
from jax.experimental.pallas import tpu as pltpu
from jax.sharding import PartitionSpec as P

RH = 32
RW = 64
BH = 8
BW = 16
LANES = 128
BLOCK_ROWS = RH // BH
BLOCK_COLS = RW // BW
REGION_BLOCKS = BLOCK_ROWS * BLOCK_COLS
PAIRS = RW // 2
BLOCK_PAIRS = BW // 2
NATURAL = RH * RW // LANES
ROWS_IN_GROUP = LANES // RW
QUADS = BH // ROWS_IN_GROUP
BF16 = jnp.bfloat16
F32 = jnp.float32


def lanes(shape):
    return lax.broadcasted_iota(jnp.int32, shape, len(shape) - 1)


def cut(value, count):
    return [value[:, v * LANES : (v + 1) * LANES] for v in range(count)]


def one_hot(depth, target):
    row = lax.broadcasted_iota(jnp.int32, (depth, target.shape[1]), 0)
    return (row == target).astype(F32).astype(BF16)


def dot(a, b):
    return jnp.dot(a, b, preferred_element_type=F32)


def pairing():
    width = BLOCK_ROWS * LANES
    n = lanes((1, width))
    parity = n // LANES
    target = n % LANES // PAIRS * LANES + parity // 2 * RW + n % PAIRS * 2 + parity % 2
    return one_hot(width, target)


def to_paired(groups, matrix):
    channels = groups[0].shape[0]
    rows = [
        jnp.concatenate([groups[QUADS * br + j] for br in range(BLOCK_ROWS)], axis=1) for j in range(QUADS)
    ]
    moved = dot(jnp.concatenate(rows, axis=0), matrix).astype(BF16)
    out = []
    for j in range(QUADS):
        here = cut(moved[j * channels : (j + 1) * channels], BLOCK_ROWS)
        for q in range(ROWS_IN_GROUP):
            out.append(jnp.concatenate(here[2 * q : 2 * q + 2], axis=0))
    return out


def unpairing():
    width = BLOCK_ROWS * LANES
    n = lanes((1, width))
    column = n % RW
    target = (n % LANES // RW * 2 + column % 2) * LANES + n // LANES * PAIRS + column // 2
    return one_hot(width, target)


def to_natural(maps, matrix):
    channels = maps[0][0].shape[0] // 2
    rows = []
    for groups in maps:
        for j in range(QUADS):
            parts = []
            for q in range(ROWS_IN_GROUP):
                group = groups[ROWS_IN_GROUP * j + q]
                parts += [group[:channels], group[channels:]]
            rows.append(jnp.concatenate(parts, axis=1))
    moved = dot(jnp.concatenate(rows, axis=0), matrix).astype(BF16)
    out = []
    for m in range(len(maps)):
        here = [
            cut(moved[(m * QUADS + j) * channels : (m * QUADS + j + 1) * channels], BLOCK_ROWS)
            for j in range(QUADS)
        ]
        out.append([here[j][br] for br in range(BLOCK_ROWS) for j in range(QUADS)])
    return out


def lane_target(source, tile):
    slot = (source // REGION_BLOCKS + tile) % 2
    return slot * LANES + source % REGION_BLOCKS * BLOCK_PAIRS


def spread(index):
    row = lax.broadcasted_iota(jnp.int32, (REGION_BLOCKS, LANES), 0)
    places = (row == lanes((REGION_BLOCKS, LANES)) // BLOCK_PAIRS).astype(F32).astype(BF16)
    rows = jnp.broadcast_to(index.astype(F32), (REGION_BLOCKS, REGION_BLOCKS)).astype(BF16)
    return dot(rows, places)


def target_of(source, tile):
    return lane_target(source.astype(jnp.int32), tile) + lanes((1, LANES)) % BLOCK_PAIRS


def put_taps(stack, i, group):
    channels = group.shape[0] // 2
    shape = (channels, LANES)
    lane = lanes(shape)
    zero = jnp.zeros(shape, BF16)
    before = jnp.where(lane % PAIRS == 0, zero, pltpu.roll(group[channels:], 1, 1))
    after = jnp.where(lane % PAIRS == PAIRS - 1, zero, pltpu.roll(group[:channels], LANES - 1, 1))
    put_rows(stack, i, (before, group[:channels], group[channels:], after))


def put_rows(stack, i, parts):
    value = jnp.concatenate(parts, axis=0)
    stack[:, (i + 1) * LANES : (i + 2) * LANES] = value
    lane = lanes(value.shape)
    zero = jnp.zeros(value.shape, BF16)
    if i == BH - 1:
        stack[:, :LANES] = jnp.where(lane < PAIRS, zero, pltpu.roll(value, PAIRS, 1))
    if i == 0:
        below = pltpu.roll(value, LANES - PAIRS, 1)
        stack[:, (BH + 1) * LANES :] = jnp.where(lane >= LANES - PAIRS, zero, below)


def picks_of(target):
    lane = lanes((1, LANES))
    before = jnp.where(lane % PAIRS == 0, -1, pltpu.roll(target, 1, 1))
    after = jnp.where(lane % PAIRS == PAIRS - 1, -1, pltpu.roll(target, LANES - 1, 1))
    depth = 2 * LANES
    return (
        one_hot(depth, jnp.concatenate([target, after], axis=1)),
        one_hot(depth, jnp.concatenate([before, target], axis=1)),
    )


def put_warped(stack, tiles, picks):
    channels = tiles[0][0].shape[0] // 2
    moved = []
    for half in range(2):
        rows = slice(half * channels, (half + 1) * channels)
        wide = [jnp.concatenate([t[i][rows] for t in tiles], axis=1) for i in range(BH)]
        moved.append(dot(jnp.concatenate(wide, axis=0), picks[half]).astype(BF16))
    for i in range(BH):
        even, odd = [m[i * channels : (i + 1) * channels] for m in moved]
        put_rows(stack, i, (odd[:, :LANES], even[:, :LANES], odd[:, LANES:], even[:, LANES:]))


def convolve(stack, weight, start=None):
    for t in (2, 4, 0, 6):
        total = None if start is None else start[:, t * LANES : (t + 2) * LANES]
        for a in range(3):
            part = dot(weight[a], stack[:, (t + a) * LANES : (t + a + 2) * LANES])
            total = part if total is None else total + part
        yield t, total[:, :LANES]
        yield t + 1, total[:, LANES:]


def lrelu(u):
    return jnp.maximum(u, 0.1 * u).astype(BF16)


def both_convolve(stacks, weights, starts):
    for here in zip(*(convolve(*operands) for operands in zip(stacks, weights, starts))):
        yield here[0][0], [u for _, u in here]


def chains(first, second, entry, starts, layers):
    both = range(2)
    nothing = (None, None)
    hidden = [[None] * BH for _ in both]
    for i, values in both_convolve(first, [entry.at[d] for d in both], starts):
        for d in both:
            hidden[d][i] = lrelu(values[d])
            put_taps(second[d], i, hidden[d][i])
    for layer in range(layers.shape[1]):
        for i, values in both_convolve(second, [layers.at[d, layer, 0] for d in both], nothing):
            for d in both:
                put_taps(first[d], i, lrelu(values[d]))
        for i, values in both_convolve(first, [layers.at[d, layer, 1] for d in both], nothing):
            for d in both:
                hidden[d][i] = (hidden[d][i].astype(F32) + values[d]).astype(BF16)
                if layer + 1 < layers.shape[1]:
                    put_taps(second[d], i, hidden[d][i])
    return hidden


def even_segment():
    return lax.axis_index("tm") % 2 == 0


def head_kernel(frames, forward_index, backward_index, payload, index, sem, index_sems):
    channels, pixels = frames.shape[-2:]
    copies = [pltpu.make_async_copy(frames.at[0, 0, 0], payload.at[:, :pixels], sem)]
    for d, source in enumerate((forward_index, backward_index)):
        copies.append(pltpu.make_async_copy(source, index.at[d], index_sems.at[d]))
    for copy in copies:
        copy.start()
    half = channels // 2
    for d in range(2):
        copies[1 + d].wait()
        source = spread(index[d, 0]).astype(BF16)
        for row in range(d * half, (d + 1) * half, REGION_BLOCKS):
            payload[row : row + REGION_BLOCKS, pixels:] = source
    copies[0].wait()


def pack_kernel(forward, backward, near_out, far_out):
    matrix = pairing()
    even = even_segment()
    packed = [to_paired(cut(source[0, 0], NATURAL), matrix) for source in (forward, backward)]
    for i, (f, b) in enumerate(zip(*packed)):
        columns = slice(i * LANES, (i + 1) * LANES)
        near_out[:, columns] = jnp.where(even, f, b)
        far_out[:, columns] = jnp.where(even, b, f)


def frame_kernel(frames, entry_frame, matrix, *rest):
    paired, parts, stack = rest
    channels = frames.shape[-2]
    for moment in range(frames.shape[0]):
        for i, group in enumerate(to_paired(cut(frames[moment, 0, 0], NATURAL), matrix[...])):
            put_taps(stack, i, group)
            paired[moment, :, i * LANES : (i + 1) * LANES] = group
        for i, group in convolve(stack, entry_frame):
            for d in range(2):
                parts[moment, d, :, i * LANES : (i + 1) * LANES] = group[
                    2 * d * channels : 2 * (d + 1) * channels
                ]


def tap_weight(taps):
    zero = jnp.zeros_like(taps[0])
    return jnp.concatenate(
        [jnp.concatenate(taps + [zero], axis=1), jnp.concatenate([zero] + taps, axis=1)], axis=0
    )


def block_diagonal(weight):
    zero = jnp.zeros_like(weight)
    return jnp.concatenate(
        [jnp.concatenate([weight, zero], axis=1), jnp.concatenate([zero, weight], axis=1)], axis=0
    )


def weights_kernel(fe, fb, be, bb, mixing, entry_frame, entry_warped, layers, mix_pair, matrix, back):
    channels = fe.shape[1]
    matrix[...] = pairing()
    back[...] = unpairing()
    for d, (entry, blocks) in enumerate(((fe, fb), (be, bb))):
        mix_pair[d] = block_diagonal(mixing[:, d * channels : (d + 1) * channels])
        for a in range(3):
            taps = [entry[3 * a + b] for b in range(3)]
            entry_frame[a, 2 * d * channels : 2 * (d + 1) * channels] = tap_weight(
                [t[:, :channels] for t in taps]
            )
            entry_warped[d, a] = tap_weight([t[:, channels:] for t in taps])
            for layer in range(blocks.shape[0]):
                for part in range(2):
                    layers[d, layer, part, a] = tap_weight(
                        [blocks[layer, part, 3 * a + b] for b in range(3)]
                    )


def picks_kernel(forward_index, backward_index, out):
    tile = lax.axis_index("tile")
    for moment in range(out.shape[0]):
        for d, index in enumerate((forward_index, backward_index)):
            for half, pick in enumerate(picks_of(target_of(spread(index[moment])[:1], tile))):
                out[moment, d, half] = pick


def by_direction(even, pair_side, other_side):
    first, second = pair_side[...], other_side[...]
    return jnp.where(even, second, first), jnp.where(even, first, second)


def near_frame_kernel(pair_frame, other_frame, entry_frame, matrix, out, picks, stack):
    even = even_segment()
    tile = lax.axis_index("tile")
    width = NATURAL * LANES
    channels = pair_frame.shape[0]
    half = channels // 2
    payloads = by_direction(even, pair_frame, other_frame)
    for d in range(2):
        for i, group in enumerate(to_paired(cut(payloads[d][:, :width], NATURAL), matrix[...])):
            put_taps(stack.at[d], i, group)
        source = payloads[d][d * half : d * half + REGION_BLOCKS, width:].astype(F32)[:1]
        for part, pick in enumerate(picks_of(target_of(source, tile))):
            picks[d, part] = pick
    for d in range(2):
        weight = [entry_frame[a, 2 * d * channels : 2 * (d + 1) * channels] for a in range(3)]
        for i, group in convolve(stack.at[d], weight):
            out[d, :, i * LANES : (i + 1) * LANES] = group


def near_kernel(
    pair_own,
    pair_swapped,
    other_own,
    other_swapped,
    starts,
    picks,
    entry_warped,
    layers,
    forward_out,
    backward_out,
    *stacks,
):
    even = even_segment()
    firsts, seconds = stacks[:2], stacks[2:]
    owns = by_direction(even, pair_own, other_own)
    others = by_direction(even, pair_swapped, other_swapped)
    for d in range(2):
        put_warped(firsts[d], (cut(owns[d], BH), cut(others[d], BH)), picks[d])
    hidden = chains(firsts, seconds, entry_warped, [starts.at[d] for d in range(2)], layers)
    for groups, out in zip(hidden, (forward_out, backward_out)):
        for i, group in enumerate(groups):
            out[:, i * LANES : (i + 1) * LANES] = group


def mix(weight, state, total):
    out = []
    for i in range(0, BH, 2):
        wide = dot(weight, jnp.concatenate(state[i : i + 2], axis=1))
        out += [total[i] + wide[:, :LANES], total[i + 1] + wide[:, LANES:]]
    return out


def rounded(groups):
    return [u.astype(BF16) for u in groups]


def put_natural(out, groups):
    for v, group in enumerate(groups):
        out[:, v * LANES : (v + 1) * LANES] = group


def tick_kernel(
    moment,
    first_own,
    first_swapped,
    second_own,
    second_swapped,
    picks,
    paired,
    parts,
    entry_warped,
    layers,
    mix_pair,
    back,
    *rest,
):
    *_, restored, forward_final, backward_final = rest[:-8] if moment > 0 else rest[:-8] + (None, None)
    *stacks, finals, mixed, final_sems, mixed_sem = rest[-8:]
    firsts, seconds = stacks[:2], stacks[2:]
    owns, others = (first_own[...], second_own[...]), (first_swapped[...], second_swapped[...])
    if moment == 0:
        even = even_segment()
        owns = by_direction(even, first_own, second_own)
        others = by_direction(even, first_swapped, second_swapped)
    for d in range(2):
        put_warped(firsts[d], (cut(owns[d], BH), cut(others[d], BH)), picks[moment, d])
    hidden = chains(firsts, seconds, entry_warped, [parts.at[moment, d] for d in range(2)], layers)
    copies = []
    for d, groups in enumerate(to_natural(hidden, back[...]) if moment > 0 else []):
        put_natural(finals.at[d], groups)
        out = (forward_final, backward_final)[d]
        copies.append(pltpu.make_async_copy(finals.at[d], out, final_sems.at[d]))
        copies[-1].start()
    total = cut(paired[moment].astype(F32), BH)
    for d in range(2):
        total = mix(mix_pair[d], hidden[d], total)
    put_natural(mixed, to_natural([rounded(total)], back[...])[0])
    copies.append(pltpu.make_async_copy(mixed, restored.at[moment], mixed_sem))
    copies[-1].start()
    for copy in copies:
        copy.wait()


VMEM = pl.BlockSpec(memory_space=pltpu.VMEM)
ANY = pl.BlockSpec(memory_space=pl.ANY)
PARAMS = pltpu.CompilerParams(vmem_limit_bytes=32 * 2**20)


def cost(flops, count):
    return pl.CostEstimate(flops=flops, bytes_accessed=count, transcendentals=0)


def head(frames, forward_source, backward_source):
    channels, pixels = frames.shape[-2:]
    return pl.pallas_call(
        head_kernel,
        out_shape=pltpu.VMEM((channels, pixels + LANES), BF16),
        in_specs=[ANY] * 3,
        out_specs=VMEM,
        scratch_shapes=[
            pltpu.VMEM((2,) + forward_source.shape, jnp.int32),
            pltpu.SemaphoreType.DMA,
            pltpu.SemaphoreType.DMA((2,)),
        ],
        compiler_params=pltpu.CompilerParams(vmem_limit_bytes=62 * 2**20),
        cost_estimate=cost(2**30, 2**19),
        name="head",
    )(frames, forward_source, backward_source)


def pack(forward, backward):
    channels, pixels = forward.shape[-2:]
    shape = jax.ShapeDtypeStruct((2 * channels, pixels // 2), BF16)
    return pl.pallas_call(
        pack_kernel,
        out_shape=(shape, shape),
        in_specs=[VMEM] * 2,
        out_specs=(VMEM, VMEM),
        compiler_params=PARAMS,
        cost_estimate=cost(2**29, 2**19),
        name="pack",
    )(forward, backward)


def pair_weights(forward_entry, forward_blocks, backward_entry, backward_blocks, mixing):
    channels = forward_entry.shape[1]
    count = forward_blocks.shape[0]
    tall, wide, square = 2 * channels, 4 * channels, BLOCK_ROWS * LANES
    shapes = (
        (3, wide, wide),
        (2, 3, tall, wide),
        (2, count, 2, 3, tall, wide),
        (2, tall, tall),
        (square, square),
        (square, square),
    )
    return pl.pallas_call(
        weights_kernel,
        out_shape=tuple(jax.ShapeDtypeStruct(shape, BF16) for shape in shapes),
        in_specs=[VMEM] * 5,
        out_specs=(VMEM,) * len(shapes),
        compiler_params=PARAMS,
        cost_estimate=cost(2**29, 2**20),
        name="pair_weights",
    )(forward_entry, forward_blocks, backward_entry, backward_blocks, mixing)


def all_picks(forward_source, backward_source):
    return pl.pallas_call(
        picks_kernel,
        out_shape=jax.ShapeDtypeStruct((forward_source.shape[0], 2, 2, 2 * LANES, 2 * LANES), BF16),
        in_specs=[VMEM] * 2,
        out_specs=VMEM,
        compiler_params=PARAMS,
        cost_estimate=cost(2**29, 2**20),
        name="all_picks",
    )(forward_source, backward_source)


def stack_of(channels):
    return pltpu.VMEM((4 * channels, (BH + 2) * LANES), BF16)


def paired_shape(frames):
    channels, pixels = frames.shape[-2:]
    return (2 * channels, pixels // 2)


def frame_parts(frames, entry_frame, matrix):
    moments = frames.shape[0]
    paired = paired_shape(frames)
    return pl.pallas_call(
        frame_kernel,
        out_shape=(
            jax.ShapeDtypeStruct((moments,) + paired, BF16),
            jax.ShapeDtypeStruct((moments, 2) + paired, F32),
        ),
        in_specs=[VMEM] * 3,
        out_specs=(VMEM, VMEM),
        scratch_shapes=[stack_of(frames.shape[-2])],
        compiler_params=PARAMS,
        cost_estimate=cost(2**31, 2**20),
        name="frame_parts",
    )(frames, entry_frame, matrix)


def near_frames(pair_frame, other_frame, entry_frame, matrix):
    channels, width = pair_frame.shape
    stack = stack_of(channels)
    return pl.pallas_call(
        near_frame_kernel,
        out_shape=(
            jax.ShapeDtypeStruct((2, 2 * channels, (width - LANES) // 2), F32),
            jax.ShapeDtypeStruct((2, 2, 2 * LANES, 2 * LANES), BF16),
        ),
        in_specs=[VMEM] * 4,
        out_specs=(VMEM, VMEM),
        scratch_shapes=[pltpu.VMEM((2,) + stack.shape, BF16)],
        compiler_params=PARAMS,
        cost_estimate=cost(2**30, 2**19),
        name="near_frames",
    )(pair_frame, other_frame, entry_frame, matrix)


def near(pair_own, *rest):
    shape = pair_own.shape
    out = jax.ShapeDtypeStruct(shape, BF16)
    stack = stack_of(shape[0] // 2)
    return pl.pallas_call(
        near_kernel,
        out_shape=(out, out),
        in_specs=[VMEM] * (1 + len(rest)),
        out_specs=(VMEM, VMEM),
        scratch_shapes=[stack] * 4,
        compiler_params=PARAMS,
        cost_estimate=cost(2**31, 2**19),
        name="near",
    )(pair_own, *rest)


def tick(moment, frames, *operands, earlier=None):
    channels, pixels = frames.shape[-2:]
    restored = jax.ShapeDtypeStruct((frames.shape[0], channels, pixels), BF16)
    state = jax.ShapeDtypeStruct((channels, pixels), BF16)
    in_specs = [VMEM] * len(operands)
    aliases = {}
    if earlier is not None:
        aliases = {len(operands): 0}
        operands += (earlier,)
        in_specs.append(ANY)
    finals = (state, state) if moment > 0 else ()
    stack = stack_of(channels)
    return pl.pallas_call(
        functools.partial(tick_kernel, moment),
        out_shape=(restored,) + finals,
        in_specs=in_specs,
        out_specs=(ANY,) * (1 + len(finals)),
        scratch_shapes=[
            *[stack] * 4,
            pltpu.VMEM((2, channels, pixels), BF16),
            pltpu.VMEM((channels, pixels), BF16),
            pltpu.SemaphoreType.DMA((2,)),
            pltpu.SemaphoreType.DMA,
        ],
        input_output_aliases=aliases,
        compiler_params=PARAMS,
        cost_estimate=cost(2**32, 2**19),
        name=f"tick_{moment}",
    )(*operands)


def sent(value, steps_even, steps_odd):
    count = lax.axis_size("tm")
    pairs = [(s, s + (steps_odd if s % 2 else steps_even)) for s in range(count)]
    return lax.ppermute(value, "tm", [(s, d) for s, d in pairs if 0 <= d < count])


def swapped(value):
    return lax.ppermute(value, "tile", [(0, 1), (1, 0)])


def later(value, *others):
    return lax.optimization_barrier((value, *others))[0]


def shards(
    frames,
    forward_carry,
    backward_carry,
    forward_source,
    backward_source,
    forward_entry,
    forward_blocks,
    backward_entry,
    backward_blocks,
    mixing_weight,
):
    payload = head(frames, forward_source, backward_source)
    pair_frame = sent(payload, 1, -1)
    near_state, far_state = pack(later(forward_carry, payload), backward_carry)
    pair_far = sent(far_state, -2, 2)
    other_far = sent(near_state, 2, -2)
    entry_frame, entry_warped, layers, mix_pair, matrix, back = pair_weights(
        later(forward_entry, near_state), forward_blocks, backward_entry, backward_blocks, mixing_weight
    )
    picks = all_picks(forward_source, backward_source)
    paired, parts = frame_parts(frames, later(entry_frame, pair_frame), matrix)
    other_frame = sent(pair_frame, 2, -2)
    pair_near = sent(near_state, 1, -1)
    other_near = sent(later(far_state, pair_frame), -1, 1)
    near_parts, near_picks = near_frames(pair_frame, other_frame, later(entry_frame, parts, picks), matrix)
    forward_one, backward_one = near(
        pair_far,
        swapped(later(pair_far, parts)),
        other_far,
        swapped(later(other_far, parts)),
        later(near_parts, pair_near, other_near),
        near_picks,
        entry_warped,
        layers,
    )
    tables = (picks, paired, parts, entry_warped, layers, mix_pair, back)
    (restored,) = tick(
        0, frames, pair_near, swapped(pair_near), other_near, swapped(other_near), *tables
    )
    restored, forward_final, backward_final = tick(
        1,
        frames,
        forward_one,
        swapped(forward_one),
        backward_one,
        swapped(backward_one),
        *tables,
        earlier=restored,
    )
    return (restored[:, None, None], forward_final[None, None], backward_final[None, None])


def solution(mesh):
    placed = (
        P(None, ("groups", "tm"), "tile", None, None),
        P(("groups", "tm"), "tile", None, None),
        P(("groups", "tm"), "tile", None, None),
        P(None, ("groups", "tm"), "tile"),
        P(None, ("groups", "tm"), "tile"),
        P(),
        P(),
        P(),
        P(),
        P(),
    )
    return jax.shard_map(
        shards,
        mesh=mesh,
        in_specs=placed,
        out_specs=(
            P(None, ("groups", "tm"), "tile", None, None),
            P(("groups", "tm"), "tile", None, None),
            P(("groups", "tm"), "tile", None, None),
        ),
        check_vma=False,
    )
```

```python
import functools

import jax
import jax.numpy as jnp
from jax import lax
from jax.experimental import pallas as pl
from jax.experimental.pallas import tpu as pltpu
from jax.sharding import PartitionSpec as P

RH = 32
RW = 64
BH = 8
BW = 16
LANES = 128
BLOCK_ROWS = RH // BH
BLOCK_COLS = RW // BW
REGION_BLOCKS = BLOCK_ROWS * BLOCK_COLS
PAIRS = RW // 2
BLOCK_PAIRS = BW // 2
NATURAL = RH * RW // LANES
ROWS_IN_GROUP = LANES // RW
QUADS = BH // ROWS_IN_GROUP
BF16 = jnp.bfloat16
F32 = jnp.float32


def lanes(shape):
    return lax.broadcasted_iota(jnp.int32, shape, len(shape) - 1)


def cut(value, count):
    return [value[:, v * LANES : (v + 1) * LANES] for v in range(count)]


def one_hot(depth, target):
    row = lax.broadcasted_iota(jnp.int32, (depth, target.shape[1]), 0)
    return (row == target).astype(F32).astype(BF16)


def dot(a, b):
    return jnp.dot(a, b, preferred_element_type=F32)


def pairing():
    width = BLOCK_ROWS * LANES
    n = lanes((1, width))
    parity = n // LANES
    target = n % LANES // PAIRS * LANES + parity // 2 * RW + n % PAIRS * 2 + parity % 2
    return one_hot(width, target)


def to_paired(groups, matrix):
    channels = groups[0].shape[0]
    rows = [
        jnp.concatenate([groups[QUADS * br + j] for br in range(BLOCK_ROWS)], axis=1) for j in range(QUADS)
    ]
    moved = dot(jnp.concatenate(rows, axis=0), matrix).astype(BF16)
    out = []
    for j in range(QUADS):
        here = cut(moved[j * channels : (j + 1) * channels], BLOCK_ROWS)
        for q in range(ROWS_IN_GROUP):
            out.append(jnp.concatenate(here[2 * q : 2 * q + 2], axis=0))
    return out


def unpairing():
    width = BLOCK_ROWS * LANES
    n = lanes((1, width))
    column = n % RW
    target = (n % LANES // RW * 2 + column % 2) * LANES + n // LANES * PAIRS + column // 2
    return one_hot(width, target)


def to_natural(maps, matrix):
    channels = maps[0][0].shape[0] // 2
    rows = []
    for groups in maps:
        for j in range(QUADS):
            parts = []
            for q in range(ROWS_IN_GROUP):
                group = groups[ROWS_IN_GROUP * j + q]
                parts += [group[:channels], group[channels:]]
            rows.append(jnp.concatenate(parts, axis=1))
    moved = dot(jnp.concatenate(rows, axis=0), matrix).astype(BF16)
    out = []
    for m in range(len(maps)):
        here = [
            cut(moved[(m * QUADS + j) * channels : (m * QUADS + j + 1) * channels], BLOCK_ROWS)
            for j in range(QUADS)
        ]
        out.append([here[j][br] for br in range(BLOCK_ROWS) for j in range(QUADS)])
    return out


def lane_target(source, tile):
    slot = (source // REGION_BLOCKS + tile) % 2
    return slot * LANES + source % REGION_BLOCKS * BLOCK_PAIRS


def spread(index):
    row = lax.broadcasted_iota(jnp.int32, (REGION_BLOCKS, LANES), 0)
    places = (row == lanes((REGION_BLOCKS, LANES)) // BLOCK_PAIRS).astype(F32).astype(BF16)
    rows = jnp.broadcast_to(index.astype(F32), (REGION_BLOCKS, REGION_BLOCKS)).astype(BF16)
    return dot(rows, places)


def target_of(source, tile):
    return lane_target(source.astype(jnp.int32), tile) + lanes((1, LANES)) % BLOCK_PAIRS


def put_taps(stack, i, group):
    channels = group.shape[0] // 2
    shape = (channels, LANES)
    lane = lanes(shape)
    zero = jnp.zeros(shape, BF16)
    before = jnp.where(lane % PAIRS == 0, zero, pltpu.roll(group[channels:], 1, 1))
    after = jnp.where(lane % PAIRS == PAIRS - 1, zero, pltpu.roll(group[:channels], LANES - 1, 1))
    put_rows(stack, i, (before, group[:channels], group[channels:], after))


def put_rows(stack, i, parts):
    value = jnp.concatenate(parts, axis=0)
    stack[:, (i + 1) * LANES : (i + 2) * LANES] = value
    lane = lanes(value.shape)
    zero = jnp.zeros(value.shape, BF16)
    if i == BH - 1:
        stack[:, :LANES] = jnp.where(lane < PAIRS, zero, pltpu.roll(value, PAIRS, 1))
    if i == 0:
        below = pltpu.roll(value, LANES - PAIRS, 1)
        stack[:, (BH + 1) * LANES :] = jnp.where(lane >= LANES - PAIRS, zero, below)


def picks_of(target):
    lane = lanes((1, LANES))
    before = jnp.where(lane % PAIRS == 0, -1, pltpu.roll(target, 1, 1))
    after = jnp.where(lane % PAIRS == PAIRS - 1, -1, pltpu.roll(target, LANES - 1, 1))
    depth = 2 * LANES
    return (
        one_hot(depth, jnp.concatenate([target, after], axis=1)),
        one_hot(depth, jnp.concatenate([before, target], axis=1)),
    )


def put_warped(stack, tiles, picks):
    channels = tiles[0][0].shape[0] // 2
    moved = []
    for half in range(2):
        rows = slice(half * channels, (half + 1) * channels)
        wide = [jnp.concatenate([t[i][rows] for t in tiles], axis=1) for i in range(BH)]
        moved.append(dot(jnp.concatenate(wide, axis=0), picks[half]).astype(BF16))
    for i in range(BH):
        even, odd = [m[i * channels : (i + 1) * channels] for m in moved]
        put_rows(stack, i, (odd[:, :LANES], even[:, :LANES], odd[:, LANES:], even[:, LANES:]))


def convolve(stack, weight, start=None):
    for t in (2, 4, 0, 6):
        total = None if start is None else start[:, t * LANES : (t + 2) * LANES]
        for a in range(3):
            part = dot(weight[a], stack[:, (t + a) * LANES : (t + a + 2) * LANES])
            total = part if total is None else total + part
        yield t, total[:, :LANES]
        yield t + 1, total[:, LANES:]


def lrelu(u):
    return jnp.maximum(u, 0.1 * u).astype(BF16)


def side_by_side(stacks, weights, starts):
    for here in zip(*(convolve(*operands) for operands in zip(stacks, weights, starts))):
        yield here[0][0], [u for _, u in here]


def chains(first, second, entries, starts, layers):
    count = range(len(first))
    nothing = [None] * len(first)
    hidden = [[None] * BH for _ in count]
    for i, values in side_by_side(first, entries, starts):
        for c in count:
            hidden[c][i] = lrelu(values[c])
            put_taps(second[c], i, hidden[c][i])
    depth = layers[0].shape[0]
    for layer in range(depth):
        for i, values in side_by_side(second, [w.at[layer, 0] for w in layers], nothing):
            for c in count:
                put_taps(first[c], i, lrelu(values[c]))
        for i, values in side_by_side(first, [w.at[layer, 1] for w in layers], nothing):
            for c in count:
                hidden[c][i] = (hidden[c][i].astype(F32) + values[c]).astype(BF16)
                if layer + 1 < depth:
                    put_taps(second[c], i, hidden[c][i])
    return hidden


def even_segment():
    return lax.axis_index("tm") % 2 == 0


def head_kernel(frames, forward_index, backward_index, payload, index, sem, index_sems):
    channels, pixels = frames.shape[-2:]
    copies = [pltpu.make_async_copy(frames.at[0, 0, 0], payload.at[:, :pixels], sem)]
    for d, source in enumerate((forward_index, backward_index)):
        copies.append(pltpu.make_async_copy(source, index.at[d], index_sems.at[d]))
    for copy in copies:
        copy.start()
    half = channels // 2
    for d in range(2):
        copies[1 + d].wait()
        source = spread(index[d, 0]).astype(BF16)
        for row in range(d * half, (d + 1) * half, REGION_BLOCKS):
            payload[row : row + REGION_BLOCKS, pixels:] = source
    copies[0].wait()


def pack_kernel(forward, backward, near_out, far_out):
    matrix = pairing()
    even = even_segment()
    packed = [to_paired(cut(source[0, 0], NATURAL), matrix) for source in (forward, backward)]
    for i, (f, b) in enumerate(zip(*packed)):
        columns = slice(i * LANES, (i + 1) * LANES)
        near_out[:, columns] = jnp.where(even, f, b)
        far_out[:, columns] = jnp.where(even, b, f)


def side_direction(pair_side):
    parity = lax.axis_index("tm") % 2
    return 1 - parity if pair_side else parity


def neighbour_part(payload, direction, entry_frame, matrix, part, picks, stack):
    channels = payload.shape[0]
    width = NATURAL * LANES
    half = channels // 2
    for i, group in enumerate(to_paired(cut(payload[:, :width], NATURAL), matrix[...])):
        put_taps(stack, i, group)
    lists = [payload[d * half : d * half + REGION_BLOCKS, width:].astype(F32)[:1] for d in range(2)]
    source = jnp.where(direction == 0, lists[0], lists[1])
    for k, pick in enumerate(picks_of(target_of(source, lax.axis_index("tile")))):
        picks[k] = pick
    rows = pl.ds(pl.multiple_of(direction * 2 * channels, 2 * channels), 2 * channels)
    for i, group in convolve(stack, [entry_frame[a, rows] for a in range(3)]):
        part[:, i * LANES : (i + 1) * LANES] = group


def frame_kernel(frames, pair_frame, entry_frame, matrix, paired, parts, pair_part, pair_picks, stack, pair_stack):
    channels = frames.shape[-2]
    for moment in range(frames.shape[0]):
        for i, group in enumerate(to_paired(cut(frames[moment, 0, 0], NATURAL), matrix[...])):
            put_taps(stack, i, group)
            paired[moment, :, i * LANES : (i + 1) * LANES] = group
        for i, group in convolve(stack, entry_frame):
            for d in range(2):
                parts[moment, d, :, i * LANES : (i + 1) * LANES] = group[
                    2 * d * channels : 2 * (d + 1) * channels
                ]
    neighbour_part(pair_frame, side_direction(True), entry_frame, matrix, pair_part, pair_picks, pair_stack)


def other_frame_kernel(other_frame, entry_frame, matrix, part, picks, stack):
    neighbour_part(other_frame, side_direction(False), entry_frame, matrix, part, picks, stack)


def tap_weight(taps):
    zero = jnp.zeros_like(taps[0])
    return jnp.concatenate(
        [jnp.concatenate(taps + [zero], axis=1), jnp.concatenate([zero] + taps, axis=1)], axis=0
    )


def block_diagonal(weight):
    zero = jnp.zeros_like(weight)
    return jnp.concatenate(
        [jnp.concatenate([weight, zero], axis=1), jnp.concatenate([zero, weight], axis=1)], axis=0
    )


def weights_kernel(fe, fb, be, bb, mixing, entry_frame, entry_warped, layers, mix_pair, matrix, back):
    channels = fe.shape[1]
    matrix[...] = pairing()
    back[...] = unpairing()
    for d, (entry, blocks) in enumerate(((fe, fb), (be, bb))):
        mix_pair[d] = block_diagonal(mixing[:, d * channels : (d + 1) * channels])
        for a in range(3):
            taps = [entry[3 * a + b] for b in range(3)]
            entry_frame[a, 2 * d * channels : 2 * (d + 1) * channels] = tap_weight(
                [t[:, :channels] for t in taps]
            )
            entry_warped[d, a] = tap_weight([t[:, channels:] for t in taps])
            for layer in range(blocks.shape[0]):
                for part in range(2):
                    layers[d, layer, part, a] = tap_weight(
                        [blocks[layer, part, 3 * a + b] for b in range(3)]
                    )


def picks_kernel(forward_index, backward_index, out):
    tile = lax.axis_index("tile")
    for moment in range(out.shape[0]):
        for d, index in enumerate((forward_index, backward_index)):
            for half, pick in enumerate(picks_of(target_of(spread(index[moment])[:1], tile))):
                out[moment, d, half] = pick


def near_kernel(
    pair_own,
    pair_swapped,
    other_own,
    other_swapped,
    pair_part,
    other_part,
    pair_picks,
    other_picks,
    entry,
    layers,
    pair_out,
    other_out,
    *stacks,
):
    firsts, seconds = stacks[:2], stacks[2:]
    directions = (side_direction(True), side_direction(False))
    for c, (tiles, picks) in enumerate(
        (((pair_own, pair_swapped), pair_picks), ((other_own, other_swapped), other_picks))
    ):
        put_warped(firsts[c], [cut(t[...], BH) for t in tiles], [picks[k] for k in range(2)])
    hidden = chains(
        firsts,
        seconds,
        [entry.at[d] for d in directions],
        [pair_part, other_part],
        [layers.at[d] for d in directions],
    )
    for groups, out in zip(hidden, (pair_out, other_out)):
        for i, group in enumerate(groups):
            out[:, i * LANES : (i + 1) * LANES] = group


def mix(weight, state, total):
    out = []
    for i in range(0, BH, 2):
        wide = dot(weight, jnp.concatenate(state[i : i + 2], axis=1))
        out += [total[i] + wide[:, :LANES], total[i + 1] + wide[:, LANES:]]
    return out


def rounded(groups):
    return [u.astype(BF16) for u in groups]


def put_natural(out, groups):
    for v, group in enumerate(groups):
        out[:, v * LANES : (v + 1) * LANES] = group


def tick_kernel(
    moment,
    pair_own,
    pair_swapped,
    other_own,
    other_swapped,
    picks,
    paired,
    parts,
    entry,
    layers,
    mix_pair,
    back,
    *rest,
):
    copies = []
    if moment > 0:
        earlier, restored, forward_final, backward_final, *stacks, finals, mixed, sems = rest
        copies.append(pltpu.make_async_copy(earlier, restored.at[0], sems.at[3]))
        copies[-1].start()
    else:
        mixed, *stacks = rest
    firsts, seconds = stacks[:2], stacks[2:]
    directions = (side_direction(True), side_direction(False))
    for c, tiles in enumerate(((pair_own, pair_swapped), (other_own, other_swapped))):
        here = [picks[moment, directions[c], k] for k in range(2)]
        put_warped(firsts[c], [cut(t[...], BH) for t in tiles], here)
    hidden = chains(
        firsts,
        seconds,
        [entry.at[d] for d in directions],
        [parts.at[moment, d] for d in directions],
        [layers.at[d] for d in directions],
    )
    for c, groups in enumerate(to_natural(hidden, back[...]) if moment > 0 else []):
        put_natural(finals.at[c], groups)
        forward_copy = pltpu.make_async_copy(finals.at[c], forward_final, sems.at[c])
        backward_copy = pltpu.make_async_copy(finals.at[c], backward_final, sems.at[c])
        pl.when(directions[c] == 0)(forward_copy.start)
        pl.when(directions[c] == 1)(backward_copy.start)
        copies.append(forward_copy)
    total = cut(paired[moment].astype(F32), BH)
    for d, state in zip(directions, hidden):
        total = mix(mix_pair[d], state, total)
    put_natural(mixed, to_natural([rounded(total)], back[...])[0])
    if moment > 0:
        copies.append(pltpu.make_async_copy(mixed, restored.at[moment], sems.at[2]))
        copies[-1].start()
    for copy in copies:
        copy.wait()


VMEM = pl.BlockSpec(memory_space=pltpu.VMEM)
ANY = pl.BlockSpec(memory_space=pl.ANY)
PARAMS = pltpu.CompilerParams(vmem_limit_bytes=32 * 2**20)


def cost(flops, count):
    return pl.CostEstimate(flops=flops, bytes_accessed=count, transcendentals=0)


def head(frames, forward_source, backward_source):
    channels, pixels = frames.shape[-2:]
    return pl.pallas_call(
        head_kernel,
        out_shape=pltpu.VMEM((channels, pixels + LANES), BF16),
        in_specs=[ANY] * 3,
        out_specs=VMEM,
        scratch_shapes=[
            pltpu.VMEM((2,) + forward_source.shape, jnp.int32),
            pltpu.SemaphoreType.DMA,
            pltpu.SemaphoreType.DMA((2,)),
        ],
        compiler_params=pltpu.CompilerParams(vmem_limit_bytes=62 * 2**20),
        cost_estimate=cost(2**30, 2**19),
        name="head",
    )(frames, forward_source, backward_source)


def pack(forward, backward):
    channels, pixels = forward.shape[-2:]
    shape = jax.ShapeDtypeStruct((2 * channels, pixels // 2), BF16)
    return pl.pallas_call(
        pack_kernel,
        out_shape=(shape, shape),
        in_specs=[VMEM] * 2,
        out_specs=(VMEM, VMEM),
        compiler_params=PARAMS,
        cost_estimate=cost(2**29, 2**19),
        name="pack",
    )(forward, backward)


def pair_weights(forward_entry, forward_blocks, backward_entry, backward_blocks, mixing):
    channels = forward_entry.shape[1]
    count = forward_blocks.shape[0]
    tall, wide, square = 2 * channels, 4 * channels, BLOCK_ROWS * LANES
    shapes = (
        (3, wide, wide),
        (2, 3, tall, wide),
        (2, count, 2, 3, tall, wide),
        (2, tall, tall),
        (square, square),
        (square, square),
    )
    return pl.pallas_call(
        weights_kernel,
        out_shape=tuple(jax.ShapeDtypeStruct(shape, BF16) for shape in shapes),
        in_specs=[VMEM] * 5,
        out_specs=(VMEM,) * len(shapes),
        compiler_params=PARAMS,
        cost_estimate=cost(2**29, 2**20),
        name="pair_weights",
    )(forward_entry, forward_blocks, backward_entry, backward_blocks, mixing)


def all_picks(forward_source, backward_source):
    return pl.pallas_call(
        picks_kernel,
        out_shape=jax.ShapeDtypeStruct((forward_source.shape[0], 2, 2, 2 * LANES, 2 * LANES), BF16),
        in_specs=[VMEM] * 2,
        out_specs=VMEM,
        compiler_params=PARAMS,
        cost_estimate=cost(2**29, 2**20),
        name="all_picks",
    )(forward_source, backward_source)


def stack_of(channels):
    return pltpu.VMEM((4 * channels, (BH + 2) * LANES), BF16)


def paired_shape(frames):
    channels, pixels = frames.shape[-2:]
    return (2 * channels, pixels // 2)


def frame_parts(frames, pair_frame, entry_frame, matrix):
    moments = frames.shape[0]
    paired = paired_shape(frames)
    stack = stack_of(frames.shape[-2])
    return pl.pallas_call(
        frame_kernel,
        out_shape=(
            jax.ShapeDtypeStruct((moments,) + paired, BF16),
            jax.ShapeDtypeStruct((moments, 2) + paired, F32),
            jax.ShapeDtypeStruct(paired, F32),
            jax.ShapeDtypeStruct((2, 2 * LANES, 2 * LANES), BF16),
        ),
        in_specs=[VMEM] * 4,
        out_specs=(VMEM,) * 4,
        scratch_shapes=[stack, stack],
        compiler_params=PARAMS,
        cost_estimate=cost(2**31, 2**20),
        name="frame_parts",
    )(frames, pair_frame, entry_frame, matrix)


def other_frame_part(other_frame, entry_frame, matrix):
    channels, width = other_frame.shape
    return pl.pallas_call(
        other_frame_kernel,
        out_shape=(
            jax.ShapeDtypeStruct((2 * channels, (width - LANES) // 2), F32),
            jax.ShapeDtypeStruct((2, 2 * LANES, 2 * LANES), BF16),
        ),
        in_specs=[VMEM] * 3,
        out_specs=(VMEM, VMEM),
        scratch_shapes=[stack_of(channels)],
        compiler_params=PARAMS,
        cost_estimate=cost(2**30, 2**19),
        name="other_frame_part",
    )(other_frame, entry_frame, matrix)


def near(pair_own, *rest):
    shape = pair_own.shape
    out = jax.ShapeDtypeStruct(shape, BF16)
    stack = stack_of(shape[0] // 2)
    return pl.pallas_call(
        near_kernel,
        out_shape=(out, out),
        in_specs=[VMEM] * (1 + len(rest)),
        out_specs=(VMEM, VMEM),
        scratch_shapes=[stack] * 4,
        compiler_params=PARAMS,
        cost_estimate=cost(2**31, 2**19),
        name="near",
    )(pair_own, *rest)


def first_tick(frames, *operands):
    stack = stack_of(frames.shape[-2])
    return pl.pallas_call(
        functools.partial(tick_kernel, 0),
        out_shape=jax.ShapeDtypeStruct(frames.shape[-2:], BF16),
        in_specs=[VMEM] * len(operands),
        out_specs=VMEM,
        scratch_shapes=[stack] * 4,
        compiler_params=PARAMS,
        cost_estimate=cost(2**32, 2**19),
        name="tick_0",
    )(*operands)


def last_tick(frames, *operands):
    shape = frames.shape[-2:]
    state = jax.ShapeDtypeStruct(shape, BF16)
    stack = stack_of(shape[0])
    return pl.pallas_call(
        functools.partial(tick_kernel, 1),
        out_shape=(jax.ShapeDtypeStruct(frames.shape[:1] + shape, BF16), state, state),
        in_specs=[VMEM] * len(operands),
        out_specs=(ANY,) * 3,
        scratch_shapes=[
            *[stack] * 4,
            pltpu.VMEM((2,) + shape, BF16),
            pltpu.VMEM(shape, BF16),
            pltpu.SemaphoreType.DMA((4,)),
        ],
        compiler_params=PARAMS,
        cost_estimate=cost(2**32, 2**19),
        name="tick_1",
    )(*operands)


def sent(value, steps_even, steps_odd):
    count = lax.axis_size("tm")
    pairs = [(s, s + (steps_odd if s % 2 else steps_even)) for s in range(count)]
    return lax.ppermute(value, "tm", [(s, d) for s, d in pairs if 0 <= d < count])


def swapped(value):
    return lax.ppermute(value, "tile", [(0, 1), (1, 0)])


def later(value, *others):
    return lax.optimization_barrier((value, *others))[0]


def shards(
    frames,
    forward_carry,
    backward_carry,
    forward_source,
    backward_source,
    forward_entry,
    forward_blocks,
    backward_entry,
    backward_blocks,
    mixing_weight,
):
    payload = head(frames, forward_source, backward_source)
    pair_frame = sent(payload, 1, -1)
    near_state, far_state = pack(later(forward_carry, payload), backward_carry)
    pair_far = sent(far_state, -2, 2)
    other_far = sent(near_state, 2, -2)
    entry_frame, entry_warped, layers, mix_pair, matrix, back = pair_weights(
        later(forward_entry, near_state), forward_blocks, backward_entry, backward_blocks, mixing_weight
    )
    picks = all_picks(forward_source, backward_source)
    paired, parts, pair_part, pair_picks = frame_parts(frames, pair_frame, entry_frame, matrix)
    other_frame = sent(pair_frame, 2, -2)
    pair_near = sent(near_state, 1, -1)
    other_near = sent(later(far_state, pair_frame), -1, 1)
    other_part, other_picks = other_frame_part(other_frame, later(entry_frame, parts, picks), matrix)
    pair_one, other_one = near(
        pair_far,
        swapped(later(pair_far, parts)),
        other_far,
        swapped(later(other_far, parts)),
        pair_part,
        later(other_part, pair_near, other_near),
        pair_picks,
        other_picks,
        entry_warped,
        layers,
    )
    tables = (picks, paired, parts, entry_warped, layers, mix_pair, back)
    first = first_tick(frames, pair_near, swapped(pair_near), other_near, swapped(other_near), *tables)
    restored, forward_final, backward_final = last_tick(
        frames, pair_one, swapped(pair_one), other_one, swapped(other_one), *tables, first
    )
    return (restored[:, None, None], forward_final[None, None], backward_final[None, None])


def solution(mesh):
    placed = (
        P(None, ("groups", "tm"), "tile", None, None),
        P(("groups", "tm"), "tile", None, None),
        P(("groups", "tm"), "tile", None, None),
        P(None, ("groups", "tm"), "tile"),
        P(None, ("groups", "tm"), "tile"),
        P(),
        P(),
        P(),
        P(),
        P(),
    )
    return jax.shard_map(
        shards,
        mesh=mesh,
        in_specs=placed,
        out_specs=(
            P(None, ("groups", "tm"), "tile", None, None),
            P(("groups", "tm"), "tile", None, None),
            P(("groups", "tm"), "tile", None, None),
        ),
        check_vma=False,
    )
```
